768 devices in a mesh: rows: 64 (over y, z_hi, core), cols: 12 (over x, z_lo).
Axes of the slice: x: 4, y: 8, z: 12 (z_hi: 4, z_lo: 3; z = z_hi * 3 + z_lo), core: 2. Of those that a mesh axis runs over, the one named last changes fastest.
Arguments:
- wind_row: float32 [64, 1024, 1536], P(None, 'rows', 'cols'), may hold values from -6 to 6
- wind_col: float32 [64, 1024, 1536], P(None, 'rows', 'cols'), may hold values from -6 to 6
- wind_up: float32 [64, 1024, 1536], P(None, 'rows', 'cols'), may hold values from -6 to 6
- pressure: float32 [64, 1024, 1536], P(None, 'rows', 'cols'), may hold values from -6 to 6
- courant: bfloat16 [64, 1024, 1536], P(None, 'rows', 'cols'), may hold values from 0.5 to 1
- stiffness: bfloat16 [64, 1024, 1536], P(None, 'rows', 'cols'), may hold values from 0.3 to 6
Outputs:
- out_row: float32 [64, 1024, 1536], P(None, 'rows', 'cols')
- out_col: float32 [64, 1024, 1536], P(None, 'rows', 'cols')
- out_up: float32 [64, 1024, 1536], P(None, 'rows', 'cols')
- out_pressure: float32 [64, 1024, 1536], P(None, 'rows', 'cols')
The draws below stay inside these ranges and needn't reach their ends.
All inputs are finite; a program needn't handle non-finite values.
Results may differ from the reference program's by a relative error of at most 0.0003.
Values sent between devices are 32-bit elements; how exact they have to be, the bound alone decides.
A program may use at most 64 MiB of HBM per device.

```python
import math
import jax
import jax.numpy as jnp
from jax import lax

LEVELS = 64
NR = 1024
NC = 1536


def draw_stiffness(key, part):
    key = jax.random.fold_in(key, 11)
    column_key, cell_key = jax.random.split(key)
    exponent = jax.random.uniform(column_key, (1, NR, NC), jnp.float32, math.log(0.6), math.log(6.0))
    column_scale = jnp.exp(exponent)
    factor = jax.random.uniform(cell_key, (LEVELS, NR, NC), jnp.float32, 0.5, 1.0)
    values = jnp.clip(column_scale * factor, 0.3, 6.0)
    return values.astype(jnp.bfloat16)


def steps_of(stream_key, shape, cuts, low, top_value):
    gain = 1.0
    for position, shards_of in cuts:
        steps = jax.random.uniform(jax.random.fold_in(jax.random.fold_in(stream_key, 6), position), (shards_of,), jnp.float32, low / len(cuts), top_value / len(cuts))
        gain = gain * jnp.repeat(jnp.exp(steps), shape[position] // shards_of).reshape((-1,) + (1,) * (len(shape) - 1 - position))
    return gain


def centred(own_key, shape, deviation, most, cuts=(), kind=jnp.bfloat16):
    drawn = jax.random.normal(own_key, shape, jnp.float32) * deviation
    if len(cuts) > 0:
        drawn = steps_of(own_key, shape, cuts, -0.22, 0.18) * drawn
    return jnp.clip(drawn, min=-most, max=most).astype(kind)


def setup_inputs(seed: int = 0) -> dict:
    arg_keys = jax.random.split(jax.random.key(seed), 7)
    return {
        "wind_row": centred(arg_keys[0], (LEVELS, NR, NC), 1.0, 6.0, ((1, 64), (2, 12)), jnp.float32),
        "wind_col": centred(arg_keys[1], (LEVELS, NR, NC), 1.0, 6.0, ((1, 64), (2, 12)), jnp.float32),
        "wind_up": centred(arg_keys[2], (LEVELS, NR, NC), 1.0, 6.0, ((1, 64), (2, 12)), jnp.float32),
        "pressure": centred(arg_keys[3], (LEVELS, NR, NC), 1.0, 6.0, ((1, 64), (2, 12)), jnp.float32),
        "courant": jnp.clip(0.5 + 0.5 * jax.random.uniform(arg_keys[4], (LEVELS, NR, NC), jnp.float32) ** steps_of(arg_keys[4], (LEVELS, NR, NC), ((1, 64), (2, 12)), -0.2, 0.2), 0.5, 1.0).astype(jnp.bfloat16),
        "stiffness": draw_stiffness(jax.random.fold_in(arg_keys[6], 71), 0),
    }


def thomas(squared, source):
    def sweep_down(carry, slab):
        upper_ratio, partial_value = carry
        weight, value = slab
        pivot = 1.0 + 2.0 * weight + weight * upper_ratio
        ratio_next = -weight / pivot
        partial_next = (value + weight * partial_value) / pivot
        return (ratio_next, partial_next), (ratio_next, partial_next)

    start = jnp.zeros_like(source[0])
    unused, (ratios, partials) = lax.scan(sweep_down, (start, start), (squared, source))

    def sweep_up(carry, slab):
        ratio, partial_value = slab
        solved = partial_value - ratio * carry
        return solved, solved

    unused, solution = lax.scan(sweep_up, start, (ratios, partials), reverse=True)
    return solution


def vertical(pressure, divergence, wind_up, courant, stiffness):
    zero_slab = jnp.zeros_like(wind_up[:1])
    below = jnp.concatenate([zero_slab, wind_up[:-1]], axis=0)
    source = pressure - courant * divergence - stiffness * (wind_up - below)
    solved = thomas(stiffness * stiffness, source)
    above = jnp.concatenate([solved[1:], zero_slab], axis=0)
    return wind_up - stiffness * (above - solved), solved


def row_ahead(field):
    return jnp.roll(field, -1, axis=1)


def row_behind(field):
    return jnp.roll(field, 1, axis=1)


def col_ahead(field):
    return jnp.concatenate([field[:, :, 1:], jnp.zeros_like(field[:, :, :1])], axis=2)


def col_behind(field):
    return jnp.concatenate([jnp.zeros_like(field[:, :, :1]), field[:, :, :-1]], axis=2)


def reference(wind_row, wind_col, wind_up, pressure, courant, stiffness):
    courant = courant.astype(jnp.float32)
    stiffness = stiffness.astype(jnp.float32)
    for substep in range(2):
        new_row = wind_row - courant * 0.5 * (row_ahead(pressure) - row_behind(pressure))
        new_col = wind_col - courant * 0.5 * (col_ahead(pressure) - col_behind(pressure))
        divergence = 0.5 * (row_ahead(new_row) - row_behind(new_row)) + 0.5 * (col_ahead(new_col) - col_behind(new_col))
        wind_up, pressure = vertical(pressure, divergence, wind_up, courant, stiffness)
        wind_row, wind_col = new_row, new_col
    return wind_row, wind_col, wind_up, pressure
```

```python
import functools

import jax
import jax.numpy as jnp
from jax import lax
from jax.experimental import pallas as pl
from jax.experimental.pallas import tpu as pltpu
from jax.sharding import PartitionSpec as P

LEVELS = 64
HALF = LEVELS // 2
ROWS = 16
LANES = 128
BASE = 8
CHUNK = 4
STEPS = HALF // CHUNK
F32 = jnp.float32


def turn(x, shift):
    return pltpu.roll(x, shift % LANES if isinstance(shift, int) else shift, x.ndim - 1)


def kernel(
    u_in, v_in, w_in, p_in, c_in, s_in,
    u_out, v_out, w_out, p_out,
    PR, UR, V, W, C16, S16, H, S, E, G, Y, M,
    RS1, RR1, RS2, RR2, CS1, CR1, CS2, CR2, OWN, EDGE, NEXT,
    in_sems, out_sems, send_sems, recv_sems,
):
    row, col = lax.axis_index("rows"), lax.axis_index("cols")
    nrow, ncol = lax.axis_size("rows"), lax.axis_size("cols")
    up, down = lax.rem(row + 1, nrow), lax.rem(row + nrow - 1, nrow)
    right, left = lax.rem(col + 1, ncol), lax.rem(col + ncol - 1, ncol)
    targets = [(up, col), (down, col), (row, right), (row, left)]

    own_rows = slice(BASE, BASE + ROWS)
    loads = [
        pltpu.make_async_copy(p_in, PR.at[pl.ds(0, LEVELS), pl.ds(BASE, ROWS), :], in_sems.at[0]),
        pltpu.make_async_copy(c_in, C16, in_sems.at[1]),
        pltpu.make_async_copy(u_in, UR.at[:, pl.ds(BASE, ROWS), :], in_sems.at[2]),
        pltpu.make_async_copy(v_in, V, in_sems.at[3]),
        pltpu.make_async_copy(s_in, S16, in_sems.at[4]),
        pltpu.make_async_copy(w_in, W.at[pl.ds(1, LEVELS)], in_sems.at[5]),
    ]
    for load in loads:
        load.start()

    barrier = pltpu.get_barrier_semaphore()
    for target in targets:
        pl.semaphore_signal(barrier, inc=1, device_id=target, device_id_type=pl.DeviceIdType.MESH)

    zero = jnp.zeros((ROWS, LANES), F32)
    W[0] = zero
    PR[LEVELS, own_rows, :] = zero

    lane = lax.broadcasted_iota(jnp.int32, (ROWS, LANES), 1)
    slot = lax.rem(lane, 4)
    group = lax.div(lane, 4)
    first_lane, last_lane = lane == 0, lane == LANES - 1
    ends = first_lane | last_lane

    for load in loads[:3]:
        load.wait()

    def halve(i, carry):
        k = pl.ds(i * 8, 8)
        H[k] = C16[k].astype(F32) * 0.5
        return carry

    lax.fori_loop(0, LEVELS // 8, halve, 0)

    p_lo, p_lo2 = PR[0:LEVELS, BASE, :], PR[0:LEVELS, BASE + 1, :]
    p_hi, p_hi2 = PR[0:LEVELS, BASE + ROWS - 1, :], PR[0:LEVELS, BASE + ROWS - 2, :]
    h_lo, h_hi = H[:, 0, :], H[:, ROWS - 1, :]
    RS1[0, 0] = p_hi
    RS1[0, 1] = UR[:, BASE + ROWS - 1, :] + h_hi * p_hi2
    RS1[0, 2] = h_hi
    RS1[1, 0] = p_lo
    RS1[1, 1] = UR[:, BASE, :] - h_lo * p_lo2
    RS1[1, 2] = h_lo

    pl.semaphore_wait(barrier, 4)

    def send(source, landing, which, direction):
        copy = pltpu.make_async_remote_copy(
            src_ref=source,
            dst_ref=landing,
            send_sem=send_sems.at[which, direction],
            recv_sem=recv_sems.at[which, direction],
            device_id=targets[direction],
            device_id_type=pl.DeviceIdType.MESH,
        )
        copy.start()
        return copy

    first = [send(RS1.at[0], RR1.at[0], 0, 0), send(RS1.at[1], RR1.at[1], 0, 1)]

    loads[3].wait()

    def pack_first(i, carry):
        out = list(carry)
        for half in range(2):
            for j in range(CHUNK):
                kappa = i * CHUNK + j
                k = half * HALF + kappa
                mask = group == kappa
                pp = turn(PR[k, own_rows, :], lax.rem(4 * kappa + 2, LANES))
                vh = jnp.where(ends, V[k], turn(H[k], 2))
                vh = turn(vh, lax.rem(4 * kappa + 1, LANES))
                out[half] = jnp.where(mask, pp, out[half])
                out[2 + half] = jnp.where(mask, vh, out[2 + half])
        return tuple(out)

    packed = lax.fori_loop(0, STEPS, pack_first, (zero, zero, zero, zero))
    for g in range(2):
        pp, vh = packed[g], packed[2 + g]
        OWN[g] = pp
        CS1[0, g] = jnp.where(slot < 2, pp, jnp.where(slot == 2, vh, turn(vh, 3)))
        CS1[1, g] = jnp.where(slot == 0, turn(vh, -3), jnp.where(slot == 1, vh, pp))
    first += [send(CS1.at[0], CR1.at[0], 0, 2), send(CS1.at[1], CR1.at[1], 0, 3)]

    loads[4].wait()

    def factor(i, carry):
        above, below = carry
        for j in range(CHUNK):
            k = i * CHUNK + j
            stiff = S16[k].astype(F32)
            S[k] = stiff
            weight = stiff * stiff
            inverse = 1.0 / (1.0 + 2.0 * weight - weight * above)
            above = weight * inverse
            E[k] = inverse
            G[k] = above
            k = LEVELS - 1 - i * CHUNK - j
            stiff = S16[k].astype(F32)
            S[k] = stiff
            weight = stiff * stiff
            inverse = 1.0 / (1.0 + 2.0 * weight - weight * below)
            below = weight * inverse
            E[k] = inverse
            G[k] = below
        return above, below

    above, below = lax.fori_loop(0, STEPS, factor, (zero, zero))
    M[...] = 1.0 / (1.0 - above * below)
    loads[5].wait()

    at_left, at_right = col == 0, col == ncol - 1
    walled = (((slot == 1) | (slot == 3)) & at_left) | (((slot == 0) | (slot == 2)) & at_right)

    def edges(g, from_left, from_right):
        own = OWN[g]
        taken = from_left * (own - turn(from_left, 2))
        v_left = from_left - turn(taken, 1)
        taken = from_right * (turn(from_right, -3) - turn(own, -1))
        v_right = from_right - turn(taken, 1)
        edge = jnp.where(
            slot == 0,
            turn(from_right, -2),
            jnp.where(slot == 1, from_left, jnp.where(slot == 2, turn(v_right, 1), v_left)),
        )
        EDGE[g] = jnp.where(walled, 0.0, edge)
        NEXT[0, g] = jnp.where(slot == 3, v_left, from_left)
        NEXT[1, g] = jnp.where(slot == 1, v_right, from_right)

    def sweep_in(i, carry):
        chain = list(carry)
        for half in range(2):
            k0 = i * CHUNK if half == 0 else LEVELS - CHUNK - i * CHUNK
            ks = pl.ds(k0, CHUNK)
            here = PR[ks, own_rows, :]
            h = H[ks]
            u1 = UR[ks, own_rows, :] - h * (
                PR[ks, BASE + 1 : BASE + ROWS + 1, :] - PR[ks, BASE - 1 : BASE + ROWS - 1, :]
            )
            UR[ks, own_rows, :] = u1
            below_edge, above_edge, v_edge = [], [], []
            for j in range(CHUNK):
                kappa = k0 + j - half * HALF
                edge = EDGE[half]
                ep = turn(edge, lax.rem(LANES + 127 - 4 * kappa, LANES))
                ev = turn(edge, lax.rem(LANES + 125 - 4 * kappa, LANES))
                k = k0 + j
                p_here = here[j]
                ahead = jnp.where(last_lane, ep, turn(p_here, -1))
                behind = jnp.where(first_lane, ep, turn(p_here, 1))
                v1 = V[k] - h[j] * (ahead - behind)
                V[k] = v1
                ahead = jnp.where(last_lane, ev, turn(v1, -1))
                behind = jnp.where(first_lane, ev, turn(v1, 1))
                v_edge.append(ahead - behind)
            du = UR[ks, BASE + 1 : BASE + ROWS + 1, :] - UR[ks, BASE - 1 : BASE + ROWS - 1, :]
            for j in range(CHUNK) if half == 0 else range(CHUNK - 1, -1, -1):
                k = k0 + j
                source = here[j] - h[j] * (du[j] + v_edge[j]) - S[k] * (W[k + 1] - W[k])
                chain[half] = E[k] * source + G[k] * chain[half]
                Y[k] = chain[half]
        return tuple(chain)

    def sweep_out(step, carry):
        q_top, q_bot, pack_top, pack_bot = carry
        for j in range(CHUNK):
            kappa = HALF - 1 - step * CHUNK - j
            q_top = Y[kappa] + G[kappa] * q_top
            PR[kappa, own_rows, :] = q_top
            pack_top = jnp.where(group == kappa, turn(q_top, lax.rem(4 * kappa + 2, LANES)), pack_top)
            kappa = step * CHUNK + j
            k = HALF + kappa
            q_bot = Y[k] + G[k] * q_bot
            PR[k, own_rows, :] = q_bot
            pack_bot = jnp.where(group == kappa, turn(q_bot, lax.rem(4 * kappa + 2, LANES)), pack_bot)
        return q_top, q_bot, pack_top, pack_bot

    def solve():
        y_top, y_bot = lax.fori_loop(0, STEPS, sweep_in, (zero, zero))
        q_bot = (y_bot + G[HALF] * y_top) * M[...]
        q_top = y_top + G[HALF - 1] * q_bot
        return lax.fori_loop(0, STEPS, sweep_out, (q_bot, q_top, zero, zero))

    def lift(i, carry):
        k0 = i * CHUNK
        W[pl.ds(k0 + 1, CHUNK)] = W[pl.ds(k0 + 1, CHUNK)] - S[pl.ds(k0, CHUNK)] * (
            PR[pl.ds(k0 + 1, CHUNK), own_rows, :] - PR[pl.ds(k0, CHUNK), own_rows, :]
        )
        return carry

    for copy in first:
        copy.wait_recv()

    PR[0:LEVELS, BASE - 1, :] = RR1[0, 0]
    PR[0:LEVELS, BASE + ROWS, :] = RR1[1, 0]
    UR[:, BASE - 1, :] = RR1[0, 1] - RR1[0, 2] * PR[0:LEVELS, BASE, :]
    UR[:, BASE + ROWS, :] = RR1[1, 1] + RR1[1, 2] * PR[0:LEVELS, BASE + ROWS - 1, :]
    for g in range(2):
        edges(g, CR1[0, g], CR1[1, g])

    unused, unused, pack_top, pack_bot = solve()

    RS2[0, 0] = PR[0:LEVELS, BASE + ROWS - 2, :]
    RS2[0, 1] = PR[0:LEVELS, BASE + ROWS - 1, :]
    RS2[1, 0] = PR[0:LEVELS, BASE + 1, :]
    RS2[1, 1] = PR[0:LEVELS, BASE, :]
    second = [send(RS2.at[0], RR2.at[0], 1, 0), send(RS2.at[1], RR2.at[1], 1, 1)]
    OWN[0] = pack_top
    OWN[1] = pack_bot
    second += [send(OWN, CR2.at[0], 1, 2), send(OWN, CR2.at[1], 1, 3)]

    lax.fori_loop(0, LEVELS // CHUNK, lift, 0)

    for copy in second:
        copy.wait_recv()

    PR[0:LEVELS, BASE - 1, :] = RR2[0, 1]
    PR[0:LEVELS, BASE + ROWS, :] = RR2[1, 1]
    UR[:, BASE - 1, :] = UR[:, BASE - 1, :] - RR1[0, 2] * (PR[0:LEVELS, BASE, :] - RR2[0, 0])
    UR[:, BASE + ROWS, :] = UR[:, BASE + ROWS, :] - RR1[1, 2] * (
        RR2[1, 0] - PR[0:LEVELS, BASE + ROWS - 1, :]
    )
    for g in range(2):
        from_left = jnp.where(slot < 2, CR2[0, g], NEXT[0, g])
        from_right = jnp.where(slot < 2, NEXT[1, g], CR2[1, g])
        edges(g, from_left, from_right)

    solve()
    stores = [
        pltpu.make_async_copy(UR.at[:, pl.ds(BASE, ROWS), :], u_out, out_sems.at[0]),
        pltpu.make_async_copy(V, v_out, out_sems.at[1]),
        pltpu.make_async_copy(PR.at[pl.ds(0, LEVELS), pl.ds(BASE, ROWS), :], p_out, out_sems.at[2]),
    ]
    for store in stores:
        store.start()
    lax.fori_loop(0, LEVELS // CHUNK, lift, 0)
    store = pltpu.make_async_copy(W.at[pl.ds(1, LEVELS)], w_out, out_sems.at[3])
    store.start()
    for copy in first + second:
        copy.wait_send()
    for store in stores + [store]:
        store.wait()


def per_device(u, v, w, p, c, s):
    block = (LEVELS, ROWS, LANES)
    padded = (LEVELS + 1, 32, LANES)
    pair = (2, ROWS, LANES)
    return pl.pallas_call(
        kernel,
        out_shape=[jax.ShapeDtypeStruct(block, F32)] * 4,
        in_specs=[pl.BlockSpec(memory_space=pl.ANY)] * 6,
        out_specs=[pl.BlockSpec(memory_space=pl.ANY)] * 4,
        scratch_shapes=[
            pltpu.VMEM(padded, F32),
            pltpu.VMEM((LEVELS, 32, LANES), F32),
            pltpu.VMEM(block, F32),
            pltpu.VMEM((LEVELS + 1, ROWS, LANES), F32),
            pltpu.VMEM(block, jnp.bfloat16),
            pltpu.VMEM(block, jnp.bfloat16),
            pltpu.VMEM(block, F32),
            pltpu.VMEM(block, F32),
            pltpu.VMEM(block, F32),
            pltpu.VMEM(block, F32),
            pltpu.VMEM(block, F32),
            pltpu.VMEM((ROWS, LANES), F32),
            pltpu.VMEM((2, 3, LEVELS, LANES), F32),
            pltpu.VMEM((2, 3, LEVELS, LANES), F32),
            pltpu.VMEM((2, 2, LEVELS, LANES), F32),
            pltpu.VMEM((2, 2, LEVELS, LANES), F32),
            pltpu.VMEM((2,) + pair, F32),
            pltpu.VMEM((2,) + pair, F32),
            pltpu.VMEM(pair, F32),
            pltpu.VMEM((2,) + pair, F32),
            pltpu.VMEM(pair, F32),
            pltpu.VMEM(pair, F32),
            pltpu.VMEM((2,) + pair, F32),
            pltpu.SemaphoreType.DMA((6,)),
            pltpu.SemaphoreType.DMA((4,)),
            pltpu.SemaphoreType.DMA((2, 4)),
            pltpu.SemaphoreType.DMA((2, 4)),
        ],
        compiler_params=pltpu.CompilerParams(
            collective_id=0, has_side_effects=True, vmem_limit_bytes=24 * 1024 * 1024
        ),
    )(u, v, w, p, c, s)


def solution(mesh):
    spec = P(None, "rows", "cols")
    return jax.shard_map(
        per_device, mesh=mesh, in_specs=(spec,) * 6, out_specs=(spec,) * 4, check_vma=False
    )
```

```python
import jax
import jax.numpy as jnp
from jax import lax
from jax.experimental import pallas as pl
from jax.experimental.pallas import tpu as pltpu
from jax.sharding import PartitionSpec as P

LEVELS = 64
HALF = LEVELS // 2
ROWS = 16
LANES = 128
BASE = 8
CHUNK = 8
STEPS = HALF // CHUNK
PARTS = 4
F32 = jnp.float32
OWN_ROWS = slice(BASE, BASE + ROWS)


def turn(x, shift):
    return pltpu.roll(x, shift % LANES if isinstance(shift, int) else shift, x.ndim - 1)


def rows_of(ref, first):
    stride = ref.shape[1]
    return ref.reshape(ref.shape[0] * stride, LANES), pl.ds(first, LEVELS, stride=stride)


def read_rows(ref, first):
    flat, rows = rows_of(ref, first)
    return flat[rows, :]


def write_rows(ref, first, value):
    flat, rows = rows_of(ref, first)
    flat[rows, :] = value


def marks():
    lane = lax.broadcasted_iota(jnp.int32, (ROWS, LANES), 1)
    return lane, lax.rem(lane, 4), lax.div(lane, 4)


def sweep_in(PR, U_old, U_new, V_old, V_new, W, H, S, E, G, EDGE, Y):
    lane = lax.broadcasted_iota(jnp.int32, (ROWS, LANES), 1)
    first_lane, last_lane = lane == 0, lane == LANES - 1
    zero = jnp.zeros((ROWS, LANES), F32)

    def body(i, carry):
        chain = list(carry)
        for half in range(2):
            k0 = i * CHUNK if half == 0 else LEVELS - CHUNK - i * CHUNK
            ks = pl.ds(k0, CHUNK)
            here = PR[ks, OWN_ROWS, :]
            h = H[ks]
            U_new[ks, OWN_ROWS, :] = U_old[ks, OWN_ROWS, :] - h * (
                PR[ks, BASE + 1 : BASE + ROWS + 1, :] - PR[ks, BASE - 1 : BASE + ROWS - 1, :]
            )
            dv = []
            for j in range(CHUNK):
                kappa = k0 + j - half * HALF
                edge = EDGE[half]
                ep = turn(edge, lax.rem(LANES + 127 - 4 * kappa, LANES))
                ev = turn(edge, lax.rem(LANES + 125 - 4 * kappa, LANES))
                k = k0 + j
                ahead = jnp.where(last_lane, ep, turn(here[j], -1))
                behind = jnp.where(first_lane, ep, turn(here[j], 1))
                v1 = V_old[k] - h[j] * (ahead - behind)
                V_new[k] = v1
                ahead = jnp.where(last_lane, ev, turn(v1, -1))
                behind = jnp.where(first_lane, ev, turn(v1, 1))
                dv.append(ahead - behind)
            du = (
                U_new[ks, BASE + 1 : BASE + ROWS + 1, :]
                - U_new[ks, BASE - 1 : BASE + ROWS - 1, :]
            )
            for j in range(CHUNK) if half == 0 else range(CHUNK - 1, -1, -1):
                k = k0 + j
                source = here[j] - h[j] * (du[j] + dv[j]) - S[k] * (W[k + 1] - W[k])
                chain[half] = E[k] * source + G[k] * chain[half]
                Y[k] = chain[half]
        return tuple(chain)

    return lax.fori_loop(0, STEPS, body, (zero, zero))


def middle(y_top, y_bot, G, M):
    q_bot = (y_bot + G[HALF] * y_top) * M[...]
    q_top = y_top + G[HALF - 1] * q_bot
    return q_bot, q_top


def exchange_kernel(
    u_in, v_in, w_in, p_in, c_in, s_in,
    PR, UR, V, W, H, S, E, G, M, EDGE,
    C16, S16, Y, RS1, RR1, RS2, RR2, CS1, CR1, CR2, OWN, NEXT,
    in_sems, send_sems, recv_sems,
):
    row, col = lax.axis_index("rows"), lax.axis_index("cols")
    nrow, ncol = lax.axis_size("rows"), lax.axis_size("cols")
    up, down = lax.rem(row + 1, nrow), lax.rem(row + nrow - 1, nrow)
    right, left = lax.rem(col + 1, ncol), lax.rem(col + ncol - 1, ncol)
    targets = [(up, col), (down, col), (row, right), (row, left)]

    barrier = pltpu.get_barrier_semaphore()
    for target in targets:
        pl.semaphore_signal(barrier, inc=1, device_id=target, device_id_type=pl.DeviceIdType.MESH)

    loads = [
        pltpu.make_async_copy(c_in, C16, in_sems.at[0]),
        pltpu.make_async_copy(p_in, PR.at[pl.ds(0, LEVELS), pl.ds(BASE, ROWS), :], in_sems.at[1]),
        pltpu.make_async_copy(u_in, UR.at[:, pl.ds(BASE, ROWS), :], in_sems.at[2]),
        pltpu.make_async_copy(v_in, V, in_sems.at[3]),
        pltpu.make_async_copy(s_in, S16, in_sems.at[4]),
        pltpu.make_async_copy(w_in, W.at[pl.ds(1, LEVELS)], in_sems.at[5]),
    ]
    for load in loads:
        load.start()

    zero = jnp.zeros((ROWS, LANES), F32)
    W[0] = zero
    PR[LEVELS, OWN_ROWS, :] = zero
    lane, slot, group = marks()
    ends = (lane == 0) | (lane == LANES - 1)

    loads[0].wait()

    def halve(i, carry):
        k = pl.ds(i * 8, 8)
        H[k] = C16[k].astype(F32) * 0.5
        return carry

    lax.fori_loop(0, LEVELS // 8, halve, 0)

    loads[1].wait()
    loads[2].wait()
    h_lo, h_hi = read_rows(H, 0), read_rows(H, ROWS - 1)
    RS1[0, 0] = read_rows(PR, BASE + ROWS - 1)
    RS1[0, 1] = read_rows(UR, BASE + ROWS - 1) + h_hi * read_rows(PR, BASE + ROWS - 2)
    RS1[0, 2] = h_hi
    RS1[1, 0] = read_rows(PR, BASE)
    RS1[1, 1] = read_rows(UR, BASE) - h_lo * read_rows(PR, BASE + 1)
    RS1[1, 2] = h_lo

    pl.semaphore_wait(barrier, 4)

    def send(source, landing, which, direction):
        copy = pltpu.make_async_remote_copy(
            src_ref=source,
            dst_ref=landing,
            send_sem=send_sems.at[which, direction],
            recv_sem=recv_sems.at[which, direction],
            device_id=targets[direction],
            device_id_type=pl.DeviceIdType.MESH,
        )
        copy.start()
        return copy

    first = [send(RS1.at[0], RR1.at[0], 0, 0), send(RS1.at[1], RR1.at[1], 0, 1)]

    loads[3].wait()

    def pack_first(i, carry):
        out = list(carry)
        for half in range(2):
            for j in range(CHUNK):
                kappa = i * CHUNK + j
                k = half * HALF + kappa
                mask = group == kappa
                pp = turn(PR[k, OWN_ROWS, :], lax.rem(4 * kappa + 2, LANES))
                vh = jnp.where(ends, V[k], turn(H[k], 2))
                vh = turn(vh, lax.rem(4 * kappa + 1, LANES))
                out[half] = jnp.where(mask, pp, out[half])
                out[2 + half] = jnp.where(mask, vh, out[2 + half])
        return tuple(out)

    packed = lax.fori_loop(0, STEPS, pack_first, (zero, zero, zero, zero))
    for g in range(2):
        pp, vh = packed[g], packed[2 + g]
        OWN[g] = pp
        CS1[0, g] = jnp.where(slot < 2, pp, jnp.where(slot == 2, vh, turn(vh, 3)))
        CS1[1, g] = jnp.where(slot == 0, turn(vh, -3), jnp.where(slot == 1, vh, pp))
    first += [send(CS1.at[0], CR1.at[0], 0, 2), send(CS1.at[1], CR1.at[1], 0, 3)]

    loads[4].wait()

    def factor(i, carry):
        above, below = carry
        for j in range(CHUNK):
            k = i * CHUNK + j
            stiff = S16[k].astype(F32)
            S[k] = stiff
            weight = stiff * stiff
            inverse = 1.0 / (1.0 + 2.0 * weight - weight * above)
            above = weight * inverse
            E[k] = inverse
            G[k] = above
            k = LEVELS - 1 - i * CHUNK - j
            stiff = S16[k].astype(F32)
            S[k] = stiff
            weight = stiff * stiff
            inverse = 1.0 / (1.0 + 2.0 * weight - weight * below)
            below = weight * inverse
            E[k] = inverse
            G[k] = below
        return above, below

    above, below = lax.fori_loop(0, STEPS, factor, (zero, zero))
    M[...] = 1.0 / (1.0 - above * below)
    loads[5].wait()

    at_left, at_right = col == 0, col == ncol - 1
    walled = (((slot == 1) | (slot == 3)) & at_left) | (((slot == 0) | (slot == 2)) & at_right)

    def edges(g, from_left, from_right):
        own = OWN[g]
        taken = from_left * (own - turn(from_left, 2))
        v_left = from_left - turn(taken, 1)
        taken = from_right * (turn(from_right, -3) - turn(own, -1))
        v_right = from_right - turn(taken, 1)
        edge = jnp.where(
            slot == 0,
            turn(from_right, -2),
            jnp.where(slot == 1, from_left, jnp.where(slot == 2, turn(v_right, 1), v_left)),
        )
        EDGE[g] = jnp.where(walled, 0.0, edge)
        return v_left, v_right

    for copy in first:
        copy.wait_recv()

    write_rows(PR, BASE - 1, RR1[0, 0])
    write_rows(PR, BASE + ROWS, RR1[1, 0])
    write_rows(UR, BASE - 1, RR1[0, 1] - RR1[0, 2] * read_rows(PR, BASE))
    write_rows(UR, BASE + ROWS, RR1[1, 1] + RR1[1, 2] * read_rows(PR, BASE + ROWS - 1))
    for g in range(2):
        from_left, from_right = CR1[0, g], CR1[1, g]
        v_left, v_right = edges(g, from_left, from_right)
        NEXT[0, g] = jnp.where(slot == 3, v_left, from_left)
        NEXT[1, g] = jnp.where(slot == 1, v_right, from_right)

    y_top, y_bot = sweep_in(PR, UR, UR, V, V, W, H, S, E, G, EDGE, Y)
    q_bot, q_top = middle(y_top, y_bot, G, M)

    def sweep_out(step, carry):
        q_top, q_bot, pack_top, pack_bot = carry
        for j in range(CHUNK):
            k = HALF - 1 - step * CHUNK - j
            q_top = Y[k] + G[k] * q_top
            PR[k, OWN_ROWS, :] = q_top
            pack_top = jnp.where(group == k, turn(q_top, lax.rem(4 * k + 2, LANES)), pack_top)
            kappa = step * CHUNK + j
            k = HALF + kappa
            q_bot = Y[k] + G[k] * q_bot
            PR[k, OWN_ROWS, :] = q_bot
            pack_bot = jnp.where(group == kappa, turn(q_bot, lax.rem(4 * kappa + 2, LANES)), pack_bot)
        return q_top, q_bot, pack_top, pack_bot

    unused, unused, pack_top, pack_bot = lax.fori_loop(
        0, STEPS, sweep_out, (q_bot, q_top, zero, zero)
    )

    RS2[0, 0] = read_rows(PR, BASE + ROWS - 2)
    RS2[0, 1] = read_rows(PR, BASE + ROWS - 1)
    RS2[1, 0] = read_rows(PR, BASE + 1)
    RS2[1, 1] = read_rows(PR, BASE)
    second = [send(RS2.at[0], RR2.at[0], 1, 0), send(RS2.at[1], RR2.at[1], 1, 1)]
    OWN[0] = pack_top
    OWN[1] = pack_bot
    second += [send(OWN, CR2.at[0], 1, 2), send(OWN, CR2.at[1], 1, 3)]

    def lift(i, carry):
        k0 = i * CHUNK
        W[pl.ds(k0 + 1, CHUNK)] = W[pl.ds(k0 + 1, CHUNK)] - S[pl.ds(k0, CHUNK)] * (
            PR[pl.ds(k0 + 1, CHUNK), OWN_ROWS, :] - PR[pl.ds(k0, CHUNK), OWN_ROWS, :]
        )
        return carry

    lax.fori_loop(0, LEVELS // CHUNK, lift, 0)

    for copy in second:
        copy.wait_recv()

    write_rows(PR, BASE - 1, RR2[0, 1])
    write_rows(PR, BASE + ROWS, RR2[1, 1])
    write_rows(
        UR, BASE - 1, read_rows(UR, BASE - 1) - RR1[0, 2] * (read_rows(PR, BASE) - RR2[0, 0])
    )
    write_rows(
        UR,
        BASE + ROWS,
        read_rows(UR, BASE + ROWS) - RR1[1, 2] * (RR2[1, 0] - read_rows(PR, BASE + ROWS - 1)),
    )
    for g in range(2):
        from_left = jnp.where(slot < 2, CR2[0, g], NEXT[0, g])
        from_right = jnp.where(slot < 2, NEXT[1, g], CR2[1, g])
        edges(g, from_left, from_right)
    for copy in first + second:
        copy.wait_send()


def finish_kernel(
    PR, UR, V, W, H, S, E, G, M, EDGE,
    u_out, v_out, w_out, p_out,
    U2, V2, W2, Q, Y, wind_sems, sems,
):
    write_rows(U2, BASE - 1, read_rows(UR, BASE - 1))
    write_rows(U2, BASE + ROWS, read_rows(UR, BASE + ROWS))
    y_top, y_bot = sweep_in(PR, UR, U2, V, V2, W, H, S, E, G, EDGE, Y)
    winds = [
        pltpu.make_async_copy(U2.at[:, pl.ds(BASE, ROWS), :], u_out, wind_sems.at[0]),
        pltpu.make_async_copy(V2, v_out, wind_sems.at[1]),
    ]
    for copy in winds:
        copy.start()
    q_bot, q_top = middle(y_top, y_bot, G, M)

    def sweep_out(step, carry):
        q_top, q_bot = carry
        for j in range(CHUNK):
            k = HALF - 1 - step * CHUNK - j
            q_next = q_top
            q_top = Y[k] + G[k] * q_next
            Q[k] = q_top
            W2[k] = W[k + 1] - S[k] * (q_next - q_top)
            k = HALF + step * CHUNK + j
            q_before = q_bot
            q_bot = Y[k] + G[k] * q_before
            Q[k] = q_bot
            W2[k - 1] = W[k] - S[k - 1] * (q_bot - q_before)
        return q_top, q_bot

    carry = q_bot, q_top
    copies = []
    part = HALF // PARTS
    for n in range(PARTS):
        carry = lax.fori_loop(n * STEPS // PARTS, (n + 1) * STEPS // PARTS, sweep_out, carry)
        low, high = HALF - (n + 1) * part, HALF + n * part
        spans = [(Q, p_out, low, low + part), (Q, p_out, high, high + part), (W2, w_out, low, low + part)]
        start, stop = max(HALF, high - 1), high + part - 1
        if n == PARTS - 1:
            W2[LEVELS - 1] = W[LEVELS] + S[LEVELS - 1] * carry[1]
            stop = LEVELS
        spans.append((W2, w_out, start, stop))
        for m, (source, target, begin, end) in enumerate(spans):
            ks = pl.ds(begin, end - begin)
            copy = pltpu.make_async_copy(source.at[ks], target.at[ks], sems.at[n, m])
            copy.start()
            copies.append(copy)
    for copy in winds + copies:
        copy.wait()


def per_device(u, v, w, p, c, s):
    block = (LEVELS, ROWS, LANES)
    padded = (LEVELS, 2 * ROWS, LANES)
    plane = (ROWS, LANES)
    pair = (2, ROWS, LANES)
    vmem = pl.BlockSpec(memory_space=pltpu.VMEM)
    hbm = pl.BlockSpec(memory_space=pltpu.HBM)
    state = [
        (LEVELS + 1, 2 * ROWS, LANES), padded, block, (LEVELS + 1, ROWS, LANES),
        block, block, block, block, plane, pair,
    ]
    held = pl.pallas_call(
        exchange_kernel,
        out_shape=[jax.ShapeDtypeStruct(shape, F32) for shape in state],
        in_specs=[hbm] * 6,
        out_specs=[vmem] * len(state),
        scratch_shapes=[
            pltpu.VMEM(block, jnp.bfloat16),
            pltpu.VMEM(block, jnp.bfloat16),
            pltpu.VMEM(block, F32),
            pltpu.VMEM((2, 3, LEVELS, LANES), F32),
            pltpu.VMEM((2, 3, LEVELS, LANES), F32),
            pltpu.VMEM((2, 2, LEVELS, LANES), F32),
            pltpu.VMEM((2, 2, LEVELS, LANES), F32),
            pltpu.VMEM((2,) + pair, F32),
            pltpu.VMEM((2,) + pair, F32),
            pltpu.VMEM((2,) + pair, F32),
            pltpu.VMEM(pair, F32),
            pltpu.VMEM((2,) + pair, F32),
            pltpu.SemaphoreType.DMA((6,)),
            pltpu.SemaphoreType.DMA((2, 4)),
            pltpu.SemaphoreType.DMA((2, 4)),
        ],
        compiler_params=pltpu.CompilerParams(
            collective_id=0, has_side_effects=True, vmem_limit_bytes=16 * 1024 * 1024
        ),
    )(*[pltpu.with_memory_space_constraint(x, pltpu.HBM) for x in (u, v, w, p, c, s)])
    return pl.pallas_call(
        finish_kernel,
        out_shape=[jax.ShapeDtypeStruct(block, F32)] * 4,
        in_specs=[vmem] * len(state),
        out_specs=[hbm] * 4,
        scratch_shapes=[
            pltpu.VMEM(padded, F32),
            pltpu.VMEM(block, F32),
            pltpu.VMEM(block, F32),
            pltpu.VMEM(block, F32),
            pltpu.VMEM(block, F32),
            pltpu.SemaphoreType.DMA((2,)),
            pltpu.SemaphoreType.DMA((PARTS, 4)),
        ],
        compiler_params=pltpu.CompilerParams(vmem_limit_bytes=16 * 1024 * 1024),
    )(*held)


def solution(mesh):
    spec = P(None, "rows", "cols")
    return jax.shard_map(
        per_device, mesh=mesh, in_specs=(spec,) * 6, out_specs=(spec,) * 4, check_vma=False
    )
```

```python
import jax
import jax.numpy as jnp
from jax import lax
from jax.experimental import pallas as pl
from jax.experimental.pallas import tpu as pltpu
from jax.sharding import PartitionSpec as P

LEVELS = 64
HALF = LEVELS // 2
ROWS = 16
LANES = 128
BASE = 8
CHUNK = 8
STEPS = HALF // CHUNK
PIECES = 2
DEPTH = HALF // PIECES
PARTS = 4
F32 = jnp.float32
OWN_ROWS = slice(BASE, BASE + ROWS)
PLANE = (ROWS, LANES)
MESH = pl.DeviceIdType.MESH


def turn(x, shift):
    return pltpu.roll(x, shift % LANES if isinstance(shift, int) else shift, x.ndim - 1)


def rows_of(ref, row, level, count):
    stride = ref.shape[1]
    return ref.reshape(ref.shape[0] * stride, LANES), pl.ds(level * stride + row, count, stride=stride)


def read_rows(ref, row, level=0, count=LEVELS):
    flat, rows = rows_of(ref, row, level, count)
    return flat[rows, :]


def write_rows(ref, row, value, level=0, count=LEVELS):
    flat, rows = rows_of(ref, row, level, count)
    flat[rows, :] = value


def edge_lanes(lane, inside):
    return (lane >= LANES - inside) | (lane < inside)


def eliminate(steps, carry, SRC, E, G, CORR, Y, V=None, VC=None, V2=None):
    lane = lax.broadcasted_iota(jnp.int32, PLANE, 1)
    near, nearest = edge_lanes(lane, 2), edge_lanes(lane, 1)

    def body(i, carry):
        chain = list(carry)
        for j in range(CHUNK):
            for half in range(2):
                k = LEVELS - 1 - i * CHUNK - j if half else i * CHUNK + j
                shift = lax.rem(2 * LANES - 4 * (k - half * HALF) - 2, LANES)
                source = SRC[k] + jnp.where(near, turn(CORR[half], shift), 0.0)
                chain[half] = E[k] * source + G[k] * chain[half]
                Y[k] = chain[half]
                if V is not None:
                    V2[k] = V[k] + jnp.where(nearest, turn(VC[half], shift), 0.0)
        return tuple(chain)

    return lax.fori_loop(*steps, body, carry)


def middle(y_top, y_bot, G, M):
    q_bot = (y_bot + G[HALF] * y_top) * M[...]
    q_top = y_top + G[HALF - 1] * q_bot
    return q_bot, q_top


def exchange_kernel(
    u_in, v_in, w_in, p_in, c_in, s_in,
    UR, V, W, S, SRC, E, G, M, CORR, VC,
    PR, H, C16, S16, Y, RS1, RR1, RS2, RR2, UH, CS1, CR1, CS2, CR2, OWN, HC, EDGE,
    in_sems, row_send1, row_recv1, col_send1, col_recv1, send2, recv2,
):
    row, col = lax.axis_index("rows"), lax.axis_index("cols")
    nrow, ncol = lax.axis_size("rows"), lax.axis_size("cols")
    up, down = lax.rem(row + 1, nrow), lax.rem(row + nrow - 1, nrow)
    right, left = lax.rem(col + 1, ncol), lax.rem(col + ncol - 1, ncol)
    targets = [(up, col), (down, col), (row, right), (row, left)]

    barrier = pltpu.get_barrier_semaphore()
    for target in targets:
        pl.semaphore_signal(barrier, inc=1, device_id=target, device_id_type=MESH)

    loads = [
        pltpu.make_async_copy(c_in, C16, in_sems.at[0]),
        pltpu.make_async_copy(p_in, PR.at[pl.ds(0, LEVELS), pl.ds(BASE, ROWS), :], in_sems.at[1]),
        pltpu.make_async_copy(u_in, UR.at[:, pl.ds(BASE, ROWS), :], in_sems.at[2]),
        pltpu.make_async_copy(v_in, V, in_sems.at[3]),
        pltpu.make_async_copy(s_in, S16, in_sems.at[4]),
        pltpu.make_async_copy(w_in, W.at[pl.ds(1, LEVELS)], in_sems.at[5]),
    ]
    for load in loads:
        load.start()

    zero = jnp.zeros(PLANE, F32)
    W[0] = zero
    PR[LEVELS, OWN_ROWS, :] = zero
    no_rows = jnp.zeros((LEVELS, LANES), F32)
    for ref in (PR, UR):
        write_rows(ref, BASE - 1, no_rows)
        write_rows(ref, BASE + ROWS, no_rows)
    lane = lax.broadcasted_iota(jnp.int32, PLANE, 1)
    slot, group = lax.rem(lane, 4), lax.div(lane, 4)
    outer, inner = (slot == 0) | (slot == 3), (slot == 1) | (slot == 2)

    loads[0].wait()

    def halve(i, carry):
        k = pl.ds(i * 8, 8)
        H[k] = C16[k].astype(F32) * 0.5
        return carry

    lax.fori_loop(0, LEVELS // 8, halve, 0)

    loads[1].wait()
    loads[2].wait()

    def send(source, landing, send_sem, recv_sem, direction):
        copy = pltpu.make_async_remote_copy(
            src_ref=source,
            dst_ref=landing,
            send_sem=send_sem,
            recv_sem=recv_sem,
            device_id=targets[direction],
            device_id_type=MESH,
        )
        copy.start()
        return copy

    def spans(n):
        return ((0, n * DEPTH), (1, LEVELS - (n + 1) * DEPTH))

    top = BASE + ROWS - 1
    row_copies = []
    for n in range(PIECES):
        for half, k0 in spans(n):
            h_lo, h_hi = read_rows(H, 0, k0, DEPTH), read_rows(H, ROWS - 1, k0, DEPTH)
            RS1[0, n, half, 0] = read_rows(PR, top, k0, DEPTH)
            RS1[0, n, half, 1] = read_rows(UR, top, k0, DEPTH) + h_hi * read_rows(PR, top - 1, k0, DEPTH)
            RS1[0, n, half, 2] = h_hi
            RS1[1, n, half, 0] = read_rows(PR, BASE, k0, DEPTH)
            RS1[1, n, half, 1] = read_rows(UR, BASE, k0, DEPTH) - h_lo * read_rows(PR, BASE + 1, k0, DEPTH)
            RS1[1, n, half, 2] = h_lo
        if n == 0:
            pl.semaphore_wait(barrier, 4)
        row_copies.append(
            [
                send(RS1.at[d, n], RR1.at[d, n], row_send1.at[d, n], row_recv1.at[d, n], d)
                for d in range(2)
            ]
        )

    loads[3].wait()

    def pack_first(i, carry):
        out = list(carry)
        for half in range(2):
            for j in range(CHUNK):
                kappa = i * CHUNK + j
                k = half * HALF + kappa
                mask = group == kappa
                shift = lax.rem(4 * kappa + 2, LANES)
                for n, field in enumerate((PR[k, OWN_ROWS, :], V[k], H[k])):
                    out[2 * n + half] = jnp.where(mask, turn(field, shift), out[2 * n + half])
        return tuple(out)

    packed = lax.fori_loop(0, STEPS, pack_first, (zero,) * 6)
    for g in range(2):
        pp, vp, hp = packed[g], packed[2 + g], packed[4 + g]
        OWN[g] = pp
        px = jnp.where(slot < 2, turn(pp, -2), turn(pp, 2))
        vx = jnp.where(slot < 2, turn(vp, -1), turn(vp, 1))
        hx = jnp.where(slot == 1, turn(hp, -1), jnp.where(slot == 2, -turn(hp, 1), 0.0))
        CS1[0, g] = jnp.where(inner, vx - hx * px, px)
        CS1[1, g] = hx
        HC[g] = jnp.where(
            slot == 0,
            hp * turn(hp, -1),
            jnp.where(slot == 1, -hp, jnp.where(slot == 2, hp, hp * turn(hp, 1))),
        )
    col_copies = [
        send(CS1, CR1.at[d], col_send1.at[d], col_recv1.at[d], 2 + d) for d in range(2)
    ]

    loads[4].wait()

    def factor(i, carry):
        ratios = list(carry)
        for j in range(CHUNK):
            for half in range(2):
                k = LEVELS - 1 - i * CHUNK - j if half else i * CHUNK + j
                stiff = S16[k].astype(F32)
                S[k] = stiff
                weight = stiff * stiff
                inverse = 1.0 / (1.0 + 2.0 * weight - weight * ratios[half])
                ratios[half] = weight * inverse
                E[k] = inverse
                G[k] = ratios[half]
        return tuple(ratios)

    above, below = lax.fori_loop(0, STEPS, factor, (zero, zero))
    M[...] = 1.0 / (1.0 - above * below)
    loads[5].wait()

    span = 4
    wide_lane = lax.broadcasted_iota(jnp.int32, (span,) + PLANE, 2)
    first_lane, last_lane = wide_lane == 0, wide_lane == LANES - 1

    def across(x):
        return jnp.where(last_lane, 0.0, turn(x, -1)) - jnp.where(first_lane, 0.0, turn(x, 1))

    def inside(i, carry):
        ks = pl.ds(i * span, span)
        here, h = PR[ks, OWN_ROWS, :], H[ks]
        UR[ks, OWN_ROWS, :] = UR[ks, OWN_ROWS, :] - h * (
            PR[ks, BASE + 1 : BASE + ROWS + 1, :] - PR[ks, BASE - 1 : BASE + ROWS - 1, :]
        )
        v_new = V[ks] - h * across(here)
        V[ks] = v_new
        du = UR[ks, BASE + 1 : BASE + ROWS + 1, :] - UR[ks, BASE - 1 : BASE + ROWS - 1, :]
        lifted = S[ks] * (W[pl.ds(i * span + 1, span)] - W[ks])
        SRC[ks] = here - h * (du + across(v_new)) - lifted
        return carry

    lax.fori_loop(0, LEVELS // span, inside, 0)

    at_left, at_right = col == 0, col == ncol - 1
    walled = ((slot >= 2) & at_left) | ((slot < 2) & at_right)

    def row_effects(k0, count, p_below, p_above, u_below, u_above):
        h_lo, h_hi = read_rows(H, 0, k0, count), read_rows(H, ROWS - 1, k0, count)
        lo, hi = h_lo * p_below, h_hi * p_above
        changes = (
            (0, h_lo * u_below),
            (1, read_rows(H, 1, k0, count) * lo),
            (ROWS - 2, read_rows(H, ROWS - 2, k0, count) * hi),
            (ROWS - 1, -h_hi * u_above),
        )
        for r, change in changes:
            write_rows(SRC, r, read_rows(SRC, r, k0, count) + change, k0, count)
        write_rows(UR, BASE, read_rows(UR, BASE, k0, count) + lo, k0, count)
        write_rows(UR, top, read_rows(UR, top, k0, count) - hi, k0, count)

    def col_effects(g, edge):
        CORR[g] = HC[g] * edge
        VC[g] = HC[g] * jnp.where(slot == 1, turn(edge, 1), turn(edge, -1))

    chain = (zero, zero)
    for n in range(PIECES):
        for copy in row_copies[n]:
            copy.wait_recv()
        for half, k0 in spans(n):
            levels = pl.ds(k0, DEPTH)
            u_below = RR1[0, n, half, 1] - RR1[0, n, half, 2] * read_rows(PR, BASE, k0, DEPTH)
            u_above = RR1[1, n, half, 1] + RR1[1, n, half, 2] * read_rows(PR, top, k0, DEPTH)
            UH[0, levels] = u_below
            UH[1, levels] = u_above
            row_effects(k0, DEPTH, RR1[0, n, half, 0], RR1[1, n, half, 0], u_below, u_above)
        if n == 0:
            for copy in col_copies:
                copy.wait_recv()
            for g in range(2):
                base = jnp.where(slot < 2, CR1[1, 0, g], CR1[0, 0, g])
                hx = jnp.where(slot < 2, CR1[1, 1, g], CR1[0, 1, g])
                edge = jnp.where(walled, 0.0, base + hx * OWN[g])
                EDGE[g] = edge
                col_effects(g, edge)
        chain = eliminate((n * STEPS // PIECES, (n + 1) * STEPS // PIECES), chain, SRC, E, G, CORR, Y)
    q_bot, q_top = middle(*chain, G, M)

    def substitute(step, carry):
        q_top, q_bot, pack_top, pack_bot = carry
        for j in range(CHUNK):
            k = HALF - 1 - step * CHUNK - j
            q_top = Y[k] + G[k] * q_top
            PR[k, OWN_ROWS, :] = q_top
            pack_top = jnp.where(group == k, turn(q_top, lax.rem(4 * k + 2, LANES)), pack_top)
            kappa = step * CHUNK + j
            k = HALF + kappa
            q_bot = Y[k] + G[k] * q_bot
            PR[k, OWN_ROWS, :] = q_bot
            pack_bot = jnp.where(group == kappa, turn(q_bot, lax.rem(4 * kappa + 2, LANES)), pack_bot)
        return q_top, q_bot, pack_top, pack_bot

    unused, unused, pack_top, pack_bot = lax.fori_loop(
        0, STEPS, substitute, (q_bot, q_top, zero, zero)
    )

    RS2[0, 0] = read_rows(PR, top - 1)
    RS2[0, 1] = read_rows(PR, top)
    RS2[1, 0] = read_rows(PR, BASE + 1)
    RS2[1, 1] = read_rows(PR, BASE)
    second = [send(RS2.at[d], RR2.at[d], send2.at[d], recv2.at[d], d) for d in range(2)]
    for g, pack in enumerate((pack_top, pack_bot)):
        OWN[g] = pack
        CS2[g] = jnp.where(slot < 2, turn(pack, -2), turn(pack, 2))
    second += [send(CS2, CR2.at[d], send2.at[2 + d], recv2.at[2 + d], 2 + d) for d in range(2)]

    nearest = edge_lanes(lane, 1)

    def settle(i, carry):
        for j in range(CHUNK):
            for half in range(2):
                kappa = i * CHUNK + j
                k = half * HALF + kappa
                shift = lax.rem(2 * LANES - 4 * kappa - 2, LANES)
                V[k] = V[k] + jnp.where(nearest, turn(VC[half], shift), 0.0)
                W[k + 1] = W[k + 1] - S[k] * (PR[k + 1, OWN_ROWS, :] - PR[k, OWN_ROWS, :])
        return carry

    lax.fori_loop(0, STEPS, settle, 0)
    lax.fori_loop(0, LEVELS // span, inside, 0)

    for copy in second:
        copy.wait_recv()

    hb, ha = [
        jnp.concatenate([RR1[d, n, half, 2] for n, half in ORDER], axis=0) for d in range(2)
    ]
    u_below = UH[0] - hb * (read_rows(PR, BASE) - RR2[0, 0])
    u_above = UH[1] + ha * (read_rows(PR, top) - RR2[1, 0])
    row_effects(0, LEVELS, RR2[0, 1], RR2[1, 1], u_below, u_above)
    for g in range(2):
        hx = jnp.where(slot < 2, CR1[1, 1, g], CR1[0, 1, g])
        qx = jnp.where(slot < 2, CR2[1, g], CR2[0, g])
        edge = jnp.where(inner, EDGE[g] + hx * (OWN[g] - qx), qx)
        col_effects(g, jnp.where(walled, 0.0, edge))
    for copy in sum(row_copies, col_copies + second):
        copy.wait_send()


ORDER = [(n, 0) for n in range(PIECES)] + [(n, 1) for n in reversed(range(PIECES))]


def finish_kernel(
    UR, V, W, S, SRC, E, G, M, CORR, VC,
    u_out, v_out, w_out, p_out,
    V2, W2, Q, Y, wind_sems, sems,
):
    winds = [
        pltpu.make_async_copy(UR.at[:, pl.ds(BASE, ROWS), :], u_out, wind_sems.at[0]),
        pltpu.make_async_copy(V2, v_out, wind_sems.at[1]),
    ]
    winds[0].start()
    zero = jnp.zeros(PLANE, F32)
    y_top, y_bot = eliminate((0, STEPS), (zero, zero), SRC, E, G, CORR, Y, V, VC, V2)
    winds[1].start()
    q_bot, q_top = middle(y_top, y_bot, G, M)

    def sweep_out(step, carry):
        q_top, q_bot = carry
        for j in range(CHUNK):
            k = HALF - 1 - step * CHUNK - j
            q_next = q_top
            q_top = Y[k] + G[k] * q_next
            Q[k] = q_top
            W2[k] = W[k + 1] - S[k] * (q_next - q_top)
            k = HALF + step * CHUNK + j
            q_before = q_bot
            q_bot = Y[k] + G[k] * q_before
            Q[k] = q_bot
            W2[k - 1] = W[k] - S[k - 1] * (q_bot - q_before)
        return q_top, q_bot

    carry = q_bot, q_top
    copies = []
    part = HALF // PARTS
    for n in range(PARTS):
        carry = lax.fori_loop(n * STEPS // PARTS, (n + 1) * STEPS // PARTS, sweep_out, carry)
        low, high = HALF - (n + 1) * part, HALF + n * part
        start, stop = max(HALF, high - 1), high + part - 1
        if n == PARTS - 1:
            W2[LEVELS - 1] = W[LEVELS] + S[LEVELS - 1] * carry[1]
            stop = LEVELS
        pieces = (
            (Q, p_out, low, low + part),
            (Q, p_out, high, high + part),
            (W2, w_out, low, low + part),
            (W2, w_out, start, stop),
        )
        for m, (source, target, begin, end) in enumerate(pieces):
            ks = pl.ds(begin, end - begin)
            copy = pltpu.make_async_copy(source.at[ks], target.at[ks], sems.at[n, m])
            copy.start()
            copies.append(copy)
    for copy in winds + copies:
        copy.wait()


def per_device(u, v, w, p, c, s):
    block = (LEVELS,) + PLANE
    deep = (LEVELS + 1,) + PLANE
    padded = (LEVELS, 2 * ROWS, LANES)
    pair = (2,) + PLANE
    vmem = pl.BlockSpec(memory_space=pltpu.VMEM)
    hbm = pl.BlockSpec(memory_space=pltpu.HBM)
    state = [padded, block, deep, block, block, block, block, PLANE, pair, pair]
    rows1 = (2, PIECES, 2, 3, DEPTH, LANES)
    rows2 = (2, 2, LEVELS, LANES)
    dma = pltpu.SemaphoreType.DMA
    held = pl.pallas_call(
        exchange_kernel,
        out_shape=[jax.ShapeDtypeStruct(shape, F32) for shape in state],
        in_specs=[hbm] * 6,
        out_specs=[vmem] * len(state),
        scratch_shapes=[
            pltpu.VMEM((LEVELS + 1, 2 * ROWS, LANES), F32),
            pltpu.VMEM(block, F32),
            pltpu.VMEM(block, jnp.bfloat16),
            pltpu.VMEM(block, jnp.bfloat16),
            pltpu.VMEM(block, F32),
            pltpu.VMEM(rows1, F32),
            pltpu.VMEM(rows1, F32),
            pltpu.VMEM(rows2, F32),
            pltpu.VMEM(rows2, F32),
            pltpu.VMEM((2, LEVELS, LANES), F32),
            pltpu.VMEM((2,) + pair, F32),
            pltpu.VMEM((2, 2) + pair, F32),
            pltpu.VMEM(pair, F32),
            pltpu.VMEM((2,) + pair, F32),
            pltpu.VMEM(pair, F32),
            pltpu.VMEM(pair, F32),
            pltpu.VMEM(pair, F32),
            dma((6,)),
            dma((2, PIECES)),
            dma((2, PIECES)),
            dma((2,)),
            dma((2,)),
            dma((4,)),
            dma((4,)),
        ],
        compiler_params=pltpu.CompilerParams(
            collective_id=0, has_side_effects=True, vmem_limit_bytes=16 * 1024 * 1024
        ),
    )(*[pltpu.with_memory_space_constraint(x, pltpu.HBM) for x in (u, v, w, p, c, s)])
    return pl.pallas_call(
        finish_kernel,
        out_shape=[jax.ShapeDtypeStruct(block, F32)] * 4,
        in_specs=[vmem] * len(state),
        out_specs=[hbm] * 4,
        scratch_shapes=[
            pltpu.VMEM(block, F32),
            pltpu.VMEM(block, F32),
            pltpu.VMEM(block, F32),
            pltpu.VMEM(block, F32),
            dma((2,)),
            dma((PARTS, 4)),
        ],
        compiler_params=pltpu.CompilerParams(vmem_limit_bytes=16 * 1024 * 1024),
    )(*held)


def solution(mesh):
    spec = P(None, "rows", "cols")
    return jax.shard_map(
        per_device, mesh=mesh, in_specs=(spec,) * 6, out_specs=(spec,) * 4, check_vma=False
    )
```

```python
import jax
import jax.numpy as jnp
from jax import lax
from jax.experimental import pallas as pl
from jax.experimental.pallas import tpu as pltpu
from jax.sharding import PartitionSpec as P

LEVELS = 64
HALF = LEVELS // 2
ROWS = 16
LANES = 128
BASE = 8
CHUNK = 8
STEPS = HALF // CHUNK
PIECES = 4
PIECES2 = 2
PARTS = 4
F32 = jnp.float32
OWN_ROWS = slice(BASE, BASE + ROWS)
PLANE = (ROWS, LANES)
MESH = pl.DeviceIdType.MESH


def turn(x, shift):
    return pltpu.roll(x, shift % LANES if isinstance(shift, int) else shift, x.ndim - 1)


def rows_of(ref, row, level, count):
    stride = ref.shape[1]
    return ref.reshape(ref.shape[0] * stride, LANES), pl.ds(level * stride + row, count, stride=stride)


def read_rows(ref, row, level=0, count=LEVELS):
    flat, rows = rows_of(ref, row, level, count)
    return flat[rows, :]


def write_rows(ref, row, value, level=0, count=LEVELS):
    flat, rows = rows_of(ref, row, level, count)
    flat[rows, :] = value


def edge_lanes(lane, inside):
    return (lane >= LANES - inside) | (lane < inside)


def eliminate(steps, carry, SRC, E, G, CORR, Y):
    lane = lax.broadcasted_iota(jnp.int32, PLANE, 1)
    near = edge_lanes(lane, 2)

    def body(i, carry):
        chain = list(carry)
        for j in range(CHUNK):
            for half in range(2):
                k = LEVELS - 1 - i * CHUNK - j if half else i * CHUNK + j
                shift = lax.rem(2 * LANES - 4 * (k - half * HALF) - 2, LANES)
                source = SRC[k] + jnp.where(near, turn(CORR[half], shift), 0.0)
                chain[half] = E[k] * source + G[k] * chain[half]
                Y[k] = chain[half]
        return tuple(chain)

    return lax.fori_loop(*steps, body, carry)


def middle(y_top, y_bot, G, M):
    q_bot = (y_bot + G[HALF] * y_top) * M[...]
    q_top = y_top + G[HALF - 1] * q_bot
    return q_bot, q_top


def exchange_kernel(
    u_in, v_in, w_in, p_in, c_in, s_in,
    UR, V, W, S, Y, G, M,
    PR, H, C16, S16, SRC, E, CORR, VC, RS1, RR1, RS2, RR2, UH, HH,
    CS1, CR1, CS2, CR2, OWN, HC, HX, EDGE,
    in_sems, row_send1, row_recv1, col_send1, col_recv1, row_send2, row_recv2, col_send2, col_recv2,
):
    row, col = lax.axis_index("rows"), lax.axis_index("cols")
    nrow, ncol = lax.axis_size("rows"), lax.axis_size("cols")
    up, down = lax.rem(row + 1, nrow), lax.rem(row + nrow - 1, nrow)
    right, left = lax.rem(col + 1, ncol), lax.rem(col + ncol - 1, ncol)
    targets = [(up, col), (down, col), (row, right), (row, left)]

    barrier = pltpu.get_barrier_semaphore()
    for target in targets:
        pl.semaphore_signal(barrier, inc=1, device_id=target, device_id_type=MESH)

    loads = [
        pltpu.make_async_copy(c_in, C16, in_sems.at[0]),
        pltpu.make_async_copy(p_in, PR.at[pl.ds(0, LEVELS), pl.ds(BASE, ROWS), :], in_sems.at[1]),
        pltpu.make_async_copy(u_in, UR.at[:, pl.ds(BASE, ROWS), :], in_sems.at[2]),
        pltpu.make_async_copy(v_in, V, in_sems.at[3]),
        pltpu.make_async_copy(s_in, S16, in_sems.at[4]),
        pltpu.make_async_copy(w_in, W.at[pl.ds(1, LEVELS)], in_sems.at[5]),
    ]
    for load in loads:
        load.start()

    zero = jnp.zeros(PLANE, F32)
    W[0] = zero
    PR[LEVELS, OWN_ROWS, :] = zero
    no_rows = jnp.zeros((LEVELS, LANES), F32)
    for ref in (PR, UR):
        write_rows(ref, BASE - 1, no_rows)
        write_rows(ref, BASE + ROWS, no_rows)
    lane = lax.broadcasted_iota(jnp.int32, PLANE, 1)
    slot, group = lax.rem(lane, 4), lax.div(lane, 4)
    outer, inner = (slot == 0) | (slot == 3), (slot == 1) | (slot == 2)

    loads[0].wait()

    def halve(i, carry):
        k = pl.ds(i * 8, 8)
        H[k] = C16[k].astype(F32) * 0.5
        return carry

    lax.fori_loop(0, LEVELS // 8, halve, 0)

    loads[1].wait()
    loads[2].wait()

    def send(source, landing, send_sem, recv_sem, direction):
        copy = pltpu.make_async_remote_copy(
            src_ref=source,
            dst_ref=landing,
            send_sem=send_sem,
            recv_sem=recv_sem,
            device_id=targets[direction],
            device_id_type=MESH,
        )
        copy.start()
        return copy

    def spans(n, depth):
        return ((0, n * depth), (1, LEVELS - (n + 1) * depth))

    top = BASE + ROWS - 1
    depth = HALF // PIECES
    for n in range(PIECES):
        for half, k0 in spans(n, depth):
            h_lo, h_hi = read_rows(H, 0, k0, depth), read_rows(H, ROWS - 1, k0, depth)
            RS1[0, n, half, 0] = read_rows(PR, top, k0, depth)
            RS1[0, n, half, 1] = read_rows(UR, top, k0, depth) + h_hi * read_rows(PR, top - 1, k0, depth)
            RS1[0, n, half, 2] = h_hi
            RS1[1, n, half, 0] = read_rows(PR, BASE, k0, depth)
            RS1[1, n, half, 1] = read_rows(UR, BASE, k0, depth) - h_lo * read_rows(PR, BASE + 1, k0, depth)
            RS1[1, n, half, 2] = h_lo

    loads[3].wait()

    def pack_first(i, carry):
        out = list(carry)
        for half in range(2):
            for j in range(CHUNK):
                kappa = i * CHUNK + j
                k = half * HALF + kappa
                mask = group == kappa
                shift = lax.rem(4 * kappa + 2, LANES)
                for n, field in enumerate((PR[k, OWN_ROWS, :], V[k], H[k])):
                    out[2 * n + half] = jnp.where(mask, turn(field, shift), out[2 * n + half])
        return tuple(out)

    packed = lax.fori_loop(0, STEPS, pack_first, (zero,) * 6)
    for g in range(2):
        pp, vp, hp = packed[g], packed[2 + g], packed[4 + g]
        OWN[g] = pp
        px = jnp.where(slot < 2, turn(pp, -2), turn(pp, 2))
        vx = jnp.where(slot < 2, turn(vp, -1), turn(vp, 1))
        hx = jnp.where(slot == 1, turn(hp, -1), jnp.where(slot == 2, -turn(hp, 1), 0.0))
        base = jnp.where(inner, vx - hx * px, px)
        CS1[0, g] = jnp.where(slot == 1, turn(hx, -1), base)
        CS1[1, g] = jnp.where(slot == 2, turn(hx, 1), base)
        HC[g] = jnp.where(
            slot == 0,
            hp * turn(hp, -1),
            jnp.where(slot == 1, -hp, jnp.where(slot == 2, hp, hp * turn(hp, 1))),
        )

    pl.semaphore_wait(barrier, 4)
    row_copies = [
        [send(RS1.at[d, n], RR1.at[d, n], row_send1.at[d, n], row_recv1.at[d, n], d) for d in range(2)]
        for n in range(PIECES)
    ]
    col_copies = [
        send(CS1.at[d], CR1.at[d], col_send1.at[d], col_recv1.at[d], 2 + d) for d in range(2)
    ]

    loads[4].wait()

    def factor(i, carry):
        ratios = list(carry)
        for j in range(CHUNK):
            for half in range(2):
                k = LEVELS - 1 - i * CHUNK - j if half else i * CHUNK + j
                stiff = S16[k].astype(F32)
                S[k] = stiff
                weight = stiff * stiff
                inverse = 1.0 / (1.0 + 2.0 * weight - weight * ratios[half])
                ratios[half] = weight * inverse
                E[k] = inverse
                G[k] = ratios[half]
        return tuple(ratios)

    above, below = lax.fori_loop(0, STEPS, factor, (zero, zero))
    M[...] = 1.0 / (1.0 - above * below)
    loads[5].wait()

    span = 4
    wide_lane = lax.broadcasted_iota(jnp.int32, (span,) + PLANE, 2)
    first_lane, last_lane = wide_lane == 0, wide_lane == LANES - 1

    def across(x):
        return jnp.where(last_lane, 0.0, turn(x, -1)) - jnp.where(first_lane, 0.0, turn(x, 1))

    def inside(i, carry):
        ks = pl.ds(i * span, span)
        here, h = PR[ks, OWN_ROWS, :], H[ks]
        UR[ks, OWN_ROWS, :] = UR[ks, OWN_ROWS, :] - h * (
            PR[ks, BASE + 1 : BASE + ROWS + 1, :] - PR[ks, BASE - 1 : BASE + ROWS - 1, :]
        )
        v_new = V[ks] - h * across(here)
        V[ks] = v_new
        du = UR[ks, BASE + 1 : BASE + ROWS + 1, :] - UR[ks, BASE - 1 : BASE + ROWS - 1, :]
        lifted = S[ks] * (W[pl.ds(i * span + 1, span)] - W[ks])
        SRC[ks] = here - h * (du + across(v_new)) - lifted
        return carry

    lax.fori_loop(0, LEVELS // span, inside, 0)

    at_left, at_right = col == 0, col == ncol - 1
    walled = ((slot >= 2) & at_left) | ((slot < 2) & at_right)

    def row_effects(k0, count, p_below, p_above, u_below, u_above):
        h_lo, h_hi = read_rows(H, 0, k0, count), read_rows(H, ROWS - 1, k0, count)
        lo, hi = h_lo * p_below, h_hi * p_above
        changes = (
            (0, h_lo * u_below),
            (1, read_rows(H, 1, k0, count) * lo),
            (ROWS - 2, read_rows(H, ROWS - 2, k0, count) * hi),
            (ROWS - 1, -h_hi * u_above),
        )
        for r, change in changes:
            write_rows(SRC, r, read_rows(SRC, r, k0, count) + change, k0, count)
        write_rows(UR, BASE, read_rows(UR, BASE, k0, count) + lo, k0, count)
        write_rows(UR, top, read_rows(UR, top, k0, count) - hi, k0, count)

    def col_effects(g, edge):
        CORR[g] = HC[g] * edge
        VC[g] = HC[g] * jnp.where(slot == 1, turn(edge, 1), turn(edge, -1))

    for copy in col_copies:
        copy.wait_recv()
    for g in range(2):
        from_left, from_right = CR1[0, g], CR1[1, g]
        base = jnp.where(slot < 2, from_right, from_left)
        hx = jnp.where(
            slot == 1, turn(from_right, -1), jnp.where(slot == 2, turn(from_left, 1), 0.0)
        )
        edge = jnp.where(walled, 0.0, base + hx * OWN[g])
        HX[g] = hx
        EDGE[g] = edge
        col_effects(g, edge)

    chain = (zero, zero)
    for n in range(PIECES):
        for copy in row_copies[n]:
            copy.wait_recv()
        for half, k0 in spans(n, depth):
            levels = pl.ds(k0, depth)
            h_below, h_above = RR1[0, n, half, 2], RR1[1, n, half, 2]
            u_below = RR1[0, n, half, 1] - h_below * read_rows(PR, BASE, k0, depth)
            u_above = RR1[1, n, half, 1] + h_above * read_rows(PR, top, k0, depth)
            UH[0, levels] = u_below
            UH[1, levels] = u_above
            HH[0, levels] = h_below
            HH[1, levels] = h_above
            row_effects(k0, depth, RR1[0, n, half, 0], RR1[1, n, half, 0], u_below, u_above)
        chain = eliminate((n * STEPS // PIECES, (n + 1) * STEPS // PIECES), chain, SRC, E, G, CORR, Y)
    q_bot, q_top = middle(*chain, G, M)

    def substitute(step, carry):
        q_top, q_bot, pack_top, pack_bot = carry
        for j in range(CHUNK):
            k = HALF - 1 - step * CHUNK - j
            q_top = Y[k] + G[k] * q_top
            PR[k, OWN_ROWS, :] = q_top
            pack_top = jnp.where(group == k, turn(q_top, lax.rem(4 * k + 2, LANES)), pack_top)
            kappa = step * CHUNK + j
            k = HALF + kappa
            q_bot = Y[k] + G[k] * q_bot
            PR[k, OWN_ROWS, :] = q_bot
            pack_bot = jnp.where(group == kappa, turn(q_bot, lax.rem(4 * kappa + 2, LANES)), pack_bot)
        return q_top, q_bot, pack_top, pack_bot

    unused, unused, pack_top, pack_bot = lax.fori_loop(
        0, STEPS, substitute, (q_bot, q_top, zero, zero)
    )

    depth2 = HALF // PIECES2
    row_copies2 = []
    for n in range(PIECES2):
        for half, k0 in spans(n, depth2):
            RS2[0, n, half, 0] = read_rows(PR, top - 1, k0, depth2)
            RS2[0, n, half, 1] = read_rows(PR, top, k0, depth2)
            RS2[1, n, half, 0] = read_rows(PR, BASE + 1, k0, depth2)
            RS2[1, n, half, 1] = read_rows(PR, BASE, k0, depth2)
        row_copies2.append(
            [
                send(RS2.at[d, n], RR2.at[d, n], row_send2.at[d, n], row_recv2.at[d, n], d)
                for d in range(2)
            ]
        )
    OWN[0] = pack_top
    OWN[1] = pack_bot
    CS2[0] = jnp.where(slot < 2, pack_bot, turn(pack_top, 2))
    CS2[1] = jnp.where(slot < 2, turn(pack_top, -2), pack_bot)
    col_copies2 = [
        send(CS2.at[d], CR2.at[d], col_send2.at[d], col_recv2.at[d], 2 + d) for d in range(2)
    ]

    nearest = edge_lanes(lane, 1)

    def settle(i, carry):
        for j in range(CHUNK):
            for half in range(2):
                kappa = i * CHUNK + j
                k = half * HALF + kappa
                shift = lax.rem(2 * LANES - 4 * kappa - 2, LANES)
                V[k] = V[k] + jnp.where(nearest, turn(VC[half], shift), 0.0)
        return carry

    def lift(i, carry):
        ks, after = pl.ds(i * span, span), pl.ds(i * span + 1, span)
        W[after] = W[after] - S[ks] * (PR[after, OWN_ROWS, :] - PR[ks, OWN_ROWS, :])
        return carry

    lax.fori_loop(0, STEPS, settle, 0)
    lax.fori_loop(0, LEVELS // span, lift, 0)
    lax.fori_loop(0, LEVELS // span, inside, 0)

    for copy in col_copies2:
        copy.wait_recv()
    from_left, from_right = CR2[0], CR2[1]
    for g in range(2):
        if g == 0:
            qx = jnp.where(slot < 2, from_right, from_left)
        else:
            qx = jnp.where(slot < 2, turn(from_right, -2), turn(from_left, 2))
        edge = jnp.where(inner, EDGE[g] + HX[g] * (OWN[g] - qx), qx)
        col_effects(g, jnp.where(walled, 0.0, edge))
    lax.fori_loop(0, STEPS, settle, 0)

    chain = (zero, zero)
    for n in range(PIECES2):
        for copy in row_copies2[n]:
            copy.wait_recv()
        for half, k0 in spans(n, depth2):
            levels = pl.ds(k0, depth2)
            q_below, q_above = RR2[0, n, half, 1], RR2[1, n, half, 1]
            u_below = UH[0, levels] - HH[0, levels] * (
                read_rows(PR, BASE, k0, depth2) - RR2[0, n, half, 0]
            )
            u_above = UH[1, levels] - HH[1, levels] * (
                RR2[1, n, half, 0] - read_rows(PR, top, k0, depth2)
            )
            row_effects(k0, depth2, q_below, q_above, u_below, u_above)
        chain = eliminate((n * STEPS // PIECES2, (n + 1) * STEPS // PIECES2), chain, SRC, E, G, CORR, Y)
    for copy in sum(row_copies + row_copies2, col_copies + col_copies2):
        copy.wait_send()


def finish_kernel(
    UR, V, W, S, Y, G, M,
    u_out, v_out, w_out, p_out,
    W2, Q, wind_sems, sems,
):
    winds = [
        pltpu.make_async_copy(UR.at[:, pl.ds(BASE, ROWS), :], u_out, wind_sems.at[0]),
        pltpu.make_async_copy(V, v_out, wind_sems.at[1]),
    ]
    for copy in winds:
        copy.start()
    q_bot, q_top = middle(Y[HALF - 1], Y[HALF], G, M)

    def sweep_out(step, carry):
        q_top, q_bot = carry
        for j in range(CHUNK):
            k = HALF - 1 - step * CHUNK - j
            q_next = q_top
            q_top = Y[k] + G[k] * q_next
            Q[k] = q_top
            W2[k] = W[k + 1] - S[k] * (q_next - q_top)
            k = HALF + step * CHUNK + j
            q_before = q_bot
            q_bot = Y[k] + G[k] * q_before
            Q[k] = q_bot
            W2[k - 1] = W[k] - S[k - 1] * (q_bot - q_before)
        return q_top, q_bot

    carry = q_bot, q_top
    copies = []
    part = HALF // PARTS
    for n in range(PARTS):
        carry = lax.fori_loop(n * STEPS // PARTS, (n + 1) * STEPS // PARTS, sweep_out, carry)
        low, high = HALF - (n + 1) * part, HALF + n * part
        start, stop = max(HALF, high - 1), high + part - 1
        if n == PARTS - 1:
            W2[LEVELS - 1] = W[LEVELS] + S[LEVELS - 1] * carry[1]
            stop = LEVELS
        pieces = (
            (Q, p_out, low, low + part),
            (Q, p_out, high, high + part),
            (W2, w_out, low, low + part),
            (W2, w_out, start, stop),
        )
        for m, (source, target, begin, end) in enumerate(pieces):
            ks = pl.ds(begin, end - begin)
            copy = pltpu.make_async_copy(source.at[ks], target.at[ks], sems.at[n, m])
            copy.start()
            copies.append(copy)
    for copy in winds + copies:
        copy.wait()


def per_device(u, v, w, p, c, s):
    block = (LEVELS,) + PLANE
    deep = (LEVELS + 1,) + PLANE
    padded = (LEVELS, 2 * ROWS, LANES)
    pair = (2,) + PLANE
    vmem = pl.BlockSpec(memory_space=pltpu.VMEM)
    hbm = pl.BlockSpec(memory_space=pltpu.HBM)
    state = [padded, block, deep, block, block, block, PLANE]
    rows1 = (2, PIECES, 2, 3, HALF // PIECES, LANES)
    rows2 = (2, PIECES2, 2, 2, HALF // PIECES2, LANES)
    halo = (2, LEVELS, LANES)
    dma = pltpu.SemaphoreType.DMA
    held = pl.pallas_call(
        exchange_kernel,
        out_shape=[jax.ShapeDtypeStruct(shape, F32) for shape in state],
        in_specs=[hbm] * 6,
        out_specs=[vmem] * len(state),
        scratch_shapes=[
            pltpu.VMEM((LEVELS + 1, 2 * ROWS, LANES), F32),
            pltpu.VMEM(block, F32),
            pltpu.VMEM(block, jnp.bfloat16),
            pltpu.VMEM(block, jnp.bfloat16),
            pltpu.VMEM(block, F32),
            pltpu.VMEM(block, F32),
            pltpu.VMEM(pair, F32),
            pltpu.VMEM(pair, F32),
            pltpu.VMEM(rows1, F32),
            pltpu.VMEM(rows1, F32),
            pltpu.VMEM(rows2, F32),
            pltpu.VMEM(rows2, F32),
            pltpu.VMEM(halo, F32),
            pltpu.VMEM(halo, F32),
            pltpu.VMEM((2,) + pair, F32),
            pltpu.VMEM((2,) + pair, F32),
            pltpu.VMEM(pair, F32),
            pltpu.VMEM(pair, F32),
            pltpu.VMEM(pair, F32),
            pltpu.VMEM(pair, F32),
            pltpu.VMEM(pair, F32),
            pltpu.VMEM(pair, F32),
            dma((6,)),
            dma((2, PIECES)),
            dma((2, PIECES)),
            dma((2,)),
            dma((2,)),
            dma((2, PIECES2)),
            dma((2, PIECES2)),
            dma((2,)),
            dma((2,)),
        ],
        compiler_params=pltpu.CompilerParams(
            collective_id=0, has_side_effects=True, vmem_limit_bytes=16 * 1024 * 1024
        ),
    )(*[pltpu.with_memory_space_constraint(x, pltpu.HBM) for x in (u, v, w, p, c, s)])
    return pl.pallas_call(
        finish_kernel,
        out_shape=[jax.ShapeDtypeStruct(block, F32)] * 4,
        in_specs=[vmem] * len(state),
        out_specs=[hbm] * 4,
        scratch_shapes=[
            pltpu.VMEM(block, F32),
            pltpu.VMEM(block, F32),
            dma((2,)),
            dma((PARTS, 4)),
        ],
        compiler_params=pltpu.CompilerParams(vmem_limit_bytes=16 * 1024 * 1024),
    )(*held)


def solution(mesh):
    spec = P(None, "rows", "cols")
    return jax.shard_map(
        per_device, mesh=mesh, in_specs=(spec,) * 6, out_specs=(spec,) * 4, check_vma=False
    )
```

```python
import jax
import jax.numpy as jnp
from jax import lax
from jax.experimental import pallas as pl
from jax.experimental.pallas import tpu as pltpu
from jax.sharding import PartitionSpec as P

LEVELS = 64
HALF = LEVELS // 2
ROWS = 16
LANES = 128
BASE = 8
CHUNK = 8
STEPS = HALF // CHUNK
PIECES = 4
PIECES2 = 2
PARTS = 2
F32 = jnp.float32
OWN_ROWS = slice(BASE, BASE + ROWS)
PLANE = (ROWS, LANES)
MESH = pl.DeviceIdType.MESH


def turn(x, shift):
    return pltpu.roll(x, shift % LANES if isinstance(shift, int) else shift, x.ndim - 1)


def rows_of(ref, row, level, count):
    stride = ref.shape[1]
    return ref.reshape(ref.shape[0] * stride, LANES), pl.ds(level * stride + row, count, stride=stride)


def read_rows(ref, row, level=0, count=LEVELS):
    flat, rows = rows_of(ref, row, level, count)
    return flat[rows, :]


def write_rows(ref, row, value, level=0, count=LEVELS):
    flat, rows = rows_of(ref, row, level, count)
    flat[rows, :] = value


def edge_lanes(lane, inside):
    return (lane >= LANES - inside) | (lane < inside)


def eliminate(steps, carry, SRC, E, G, CORR, Y):
    lane = lax.broadcasted_iota(jnp.int32, PLANE, 1)
    near = edge_lanes(lane, 2)

    def body(i, carry):
        chain = list(carry)
        for j in range(CHUNK):
            for half in range(2):
                k = LEVELS - 1 - i * CHUNK - j if half else i * CHUNK + j
                shift = lax.rem(2 * LANES - 4 * (k - half * HALF) - 2, LANES)
                source = SRC[k] + jnp.where(near, turn(CORR[half], shift), 0.0)
                chain[half] = E[k] * source + G[k] * chain[half]
                Y[k] = chain[half]
        return tuple(chain)

    return lax.fori_loop(*steps, body, carry)


def middle(y_top, y_bot, G, M):
    q_bot = (y_bot + G[HALF] * y_top) * M[...]
    q_top = y_top + G[HALF - 1] * q_bot
    return q_bot, q_top


def exchange_kernel(
    u_in, v_in, w_in, p_in, c_in, s_in,
    UR, V, W, S, Y, G, M, VC,
    PR, H, C16, S16, SRC, E, CORR, RS1, RR1, RS2, RR2, UH, HH,
    CS1, CR1, CS2, CR2, OWN, HC, HX, EDGE,
    in_sems, row_send1, row_recv1, col_send1, col_recv1, row_send2, row_recv2, col_send2, col_recv2,
):
    row, col = lax.axis_index("rows"), lax.axis_index("cols")
    nrow, ncol = lax.axis_size("rows"), lax.axis_size("cols")
    up, down = lax.rem(row + 1, nrow), lax.rem(row + nrow - 1, nrow)
    right, left = lax.rem(col + 1, ncol), lax.rem(col + ncol - 1, ncol)
    targets = [(up, col), (down, col), (row, right), (row, left)]
    away = 1 - lax.rem(row, 2)

    barrier = pltpu.get_barrier_semaphore()
    for target in targets:
        pl.semaphore_signal(barrier, inc=1, device_id=target, device_id_type=MESH)

    loads = [
        pltpu.make_async_copy(c_in, C16, in_sems.at[0]),
        pltpu.make_async_copy(p_in, PR.at[pl.ds(0, LEVELS), pl.ds(BASE, ROWS), :], in_sems.at[1]),
        pltpu.make_async_copy(u_in, UR.at[:, pl.ds(BASE, ROWS), :], in_sems.at[2]),
        pltpu.make_async_copy(v_in, V, in_sems.at[3]),
        pltpu.make_async_copy(s_in, S16, in_sems.at[4]),
        pltpu.make_async_copy(w_in, W.at[pl.ds(1, LEVELS)], in_sems.at[5]),
    ]
    for load in loads:
        load.start()

    zero = jnp.zeros(PLANE, F32)
    W[0] = zero
    PR[LEVELS, OWN_ROWS, :] = zero
    no_rows = jnp.zeros((LEVELS, LANES), F32)
    for ref in (PR, UR):
        write_rows(ref, BASE - 1, no_rows)
        write_rows(ref, BASE + ROWS, no_rows)
    lane = lax.broadcasted_iota(jnp.int32, PLANE, 1)
    slot, group = lax.rem(lane, 4), lax.div(lane, 4)
    outer, inner = (slot == 0) | (slot == 3), (slot == 1) | (slot == 2)

    loads[0].wait()

    def halve(i, carry):
        k = pl.ds(i * 8, 8)
        H[k] = C16[k].astype(F32) * 0.5
        return carry

    lax.fori_loop(0, LEVELS // 8, halve, 0)

    loads[1].wait()
    loads[2].wait()

    def remote(source, landing, send_sem, recv_sem, target):
        return pltpu.make_async_remote_copy(
            src_ref=source,
            dst_ref=landing,
            send_sem=send_sem,
            recv_sem=recv_sem,
            device_id=target,
            device_id_type=MESH,
        )

    def row_copy(source, landing, send_sem, recv_sem, d, n):
        target = (lax.rem(row + nrow + 1 - 2 * d, nrow), col)
        return remote(source.at[d, n], landing.at[d, n], send_sem.at[d, n], recv_sem.at[d, n], target)

    def col_copy(source, landing, send_sem, recv_sem, d):
        return remote(source.at[d], landing.at[d], send_sem.at[d], recv_sem.at[d], targets[2 + d])

    def spans(n, depth):
        return ((0, n * depth), (1, LEVELS - (n + 1) * depth))

    top = BASE + ROWS - 1
    depth = HALF // PIECES
    for n in range(PIECES):
        for half, k0 in spans(n, depth):
            h_lo, h_hi = read_rows(H, 0, k0, depth), read_rows(H, ROWS - 1, k0, depth)
            RS1[0, n, half, 0] = read_rows(PR, top, k0, depth)
            RS1[0, n, half, 1] = read_rows(UR, top, k0, depth) + h_hi * read_rows(PR, top - 1, k0, depth)
            RS1[0, n, half, 2] = h_hi
            RS1[1, n, half, 0] = read_rows(PR, BASE, k0, depth)
            RS1[1, n, half, 1] = read_rows(UR, BASE, k0, depth) - h_lo * read_rows(PR, BASE + 1, k0, depth)
            RS1[1, n, half, 2] = h_lo

    loads[3].wait()

    def pack_first(i, carry):
        out = list(carry)
        for half in range(2):
            for j in range(CHUNK):
                kappa = i * CHUNK + j
                k = half * HALF + kappa
                mask = group == kappa
                shift = lax.rem(4 * kappa + 2, LANES)
                for n, field in enumerate((PR[k, OWN_ROWS, :], V[k], H[k])):
                    out[2 * n + half] = jnp.where(mask, turn(field, shift), out[2 * n + half])
        return tuple(out)

    packed = lax.fori_loop(0, STEPS, pack_first, (zero,) * 6)
    for g in range(2):
        pp, vp, hp = packed[g], packed[2 + g], packed[4 + g]
        OWN[g] = pp
        px = jnp.where(slot < 2, turn(pp, -2), turn(pp, 2))
        vx = jnp.where(slot < 2, turn(vp, -1), turn(vp, 1))
        hx = jnp.where(slot == 1, turn(hp, -1), jnp.where(slot == 2, -turn(hp, 1), 0.0))
        base = jnp.where(inner, vx - hx * px, px)
        CS1[0, g] = jnp.where(slot == 1, turn(hx, -1), base)
        CS1[1, g] = jnp.where(slot == 2, turn(hx, 1), base)
        HC[g] = jnp.where(
            slot == 0,
            hp * turn(hp, -1),
            jnp.where(slot == 1, -hp, jnp.where(slot == 2, hp, hp * turn(hp, 1))),
        )

    pl.semaphore_wait(barrier, 4)
    rows1 = (RS1, RR1, row_send1, row_recv1)
    row_copies = [[row_copy(*rows1, d, n) for d in range(2)] for n in range(PIECES)]
    col_copies = [col_copy(CS1, CR1, col_send1, col_recv1, d) for d in range(2)]
    for n in range(PIECES):
        row_copy(*rows1, away, n).start()
    for copy in col_copies:
        copy.start()
    for n in range(PIECES):
        row_copy(*rows1, 1 - away, n).start()

    loads[4].wait()

    def factor(i, carry):
        ratios = list(carry)
        for j in range(CHUNK):
            for half in range(2):
                k = LEVELS - 1 - i * CHUNK - j if half else i * CHUNK + j
                stiff = S16[k].astype(F32)
                S[k] = stiff
                weight = stiff * stiff
                inverse = 1.0 / (1.0 + 2.0 * weight - weight * ratios[half])
                ratios[half] = weight * inverse
                E[k] = inverse
                G[k] = ratios[half]
        return tuple(ratios)

    above, below = lax.fori_loop(0, STEPS, factor, (zero, zero))
    M[...] = 1.0 / (1.0 - above * below)
    loads[5].wait()

    span = 4
    wide_lane = lax.broadcasted_iota(jnp.int32, (span,) + PLANE, 2)
    first_lane, last_lane = wide_lane == 0, wide_lane == LANES - 1

    def across(x):
        return jnp.where(last_lane, 0.0, turn(x, -1)) - jnp.where(first_lane, 0.0, turn(x, 1))

    def inside(i, carry):
        ks = pl.ds(i * span, span)
        here, h = PR[ks, OWN_ROWS, :], H[ks]
        UR[ks, OWN_ROWS, :] = UR[ks, OWN_ROWS, :] - h * (
            PR[ks, BASE + 1 : BASE + ROWS + 1, :] - PR[ks, BASE - 1 : BASE + ROWS - 1, :]
        )
        v_new = V[ks] - h * across(here)
        V[ks] = v_new
        du = UR[ks, BASE + 1 : BASE + ROWS + 1, :] - UR[ks, BASE - 1 : BASE + ROWS - 1, :]
        lifted = S[ks] * (W[pl.ds(i * span + 1, span)] - W[ks])
        SRC[ks] = here - h * (du + across(v_new)) - lifted
        return carry

    lax.fori_loop(0, LEVELS // span, inside, 0)

    at_left, at_right = col == 0, col == ncol - 1
    walled = ((slot >= 2) & at_left) | ((slot < 2) & at_right)

    def row_effects(k0, count, p_below, p_above, u_below, u_above):
        h_lo, h_hi = read_rows(H, 0, k0, count), read_rows(H, ROWS - 1, k0, count)
        lo, hi = h_lo * p_below, h_hi * p_above
        changes = (
            (0, h_lo * u_below),
            (1, read_rows(H, 1, k0, count) * lo),
            (ROWS - 2, read_rows(H, ROWS - 2, k0, count) * hi),
            (ROWS - 1, -h_hi * u_above),
        )
        for r, change in changes:
            write_rows(SRC, r, read_rows(SRC, r, k0, count) + change, k0, count)
        write_rows(UR, BASE, read_rows(UR, BASE, k0, count) + lo, k0, count)
        write_rows(UR, top, read_rows(UR, top, k0, count) - hi, k0, count)

    def col_effects(g, edge):
        CORR[g] = HC[g] * edge
        VC[g] = HC[g] * jnp.where(slot == 1, turn(edge, 1), turn(edge, -1))

    for copy in col_copies:
        copy.wait_recv()
    for g in range(2):
        from_left, from_right = CR1[0, g], CR1[1, g]
        base = jnp.where(slot < 2, from_right, from_left)
        hx = jnp.where(
            slot == 1, turn(from_right, -1), jnp.where(slot == 2, turn(from_left, 1), 0.0)
        )
        edge = jnp.where(walled, 0.0, base + hx * OWN[g])
        HX[g] = hx
        EDGE[g] = edge
        col_effects(g, edge)

    chain = (zero, zero)
    for n in range(PIECES):
        for copy in row_copies[n]:
            copy.wait_recv()
        for half, k0 in spans(n, depth):
            levels = pl.ds(k0, depth)
            h_below, h_above = RR1[0, n, half, 2], RR1[1, n, half, 2]
            u_below = RR1[0, n, half, 1] - h_below * read_rows(PR, BASE, k0, depth)
            u_above = RR1[1, n, half, 1] + h_above * read_rows(PR, top, k0, depth)
            UH[0, levels] = u_below
            UH[1, levels] = u_above
            HH[0, levels] = h_below
            HH[1, levels] = h_above
            row_effects(k0, depth, RR1[0, n, half, 0], RR1[1, n, half, 0], u_below, u_above)
        chain = eliminate((n * STEPS // PIECES, (n + 1) * STEPS // PIECES), chain, SRC, E, G, CORR, Y)
    q_bot, q_top = middle(*chain, G, M)

    def substitute(step, carry):
        q_top, q_bot, pack_top, pack_bot = carry
        for j in range(CHUNK):
            k = HALF - 1 - step * CHUNK - j
            q_top = Y[k] + G[k] * q_top
            PR[k, OWN_ROWS, :] = q_top
            pack_top = jnp.where(group == k, turn(q_top, lax.rem(4 * k + 2, LANES)), pack_top)
            kappa = step * CHUNK + j
            k = HALF + kappa
            q_bot = Y[k] + G[k] * q_bot
            PR[k, OWN_ROWS, :] = q_bot
            pack_bot = jnp.where(group == kappa, turn(q_bot, lax.rem(4 * kappa + 2, LANES)), pack_bot)
        return q_top, q_bot, pack_top, pack_bot

    unused, unused, pack_top, pack_bot = lax.fori_loop(
        0, STEPS, substitute, (q_bot, q_top, zero, zero)
    )

    depth2 = HALF // PIECES2
    rows2 = (RS2, RR2, row_send2, row_recv2)
    row_copies2 = [[row_copy(*rows2, d, n) for d in range(2)] for n in range(PIECES2)]
    col_copies2 = [col_copy(CS2, CR2, col_send2, col_recv2, d) for d in range(2)]
    for n in range(PIECES2):
        for half, k0 in spans(n, depth2):
            RS2[0, n, half, 0] = read_rows(PR, top - 1, k0, depth2)
            RS2[0, n, half, 1] = read_rows(PR, top, k0, depth2)
            RS2[1, n, half, 0] = read_rows(PR, BASE + 1, k0, depth2)
            RS2[1, n, half, 1] = read_rows(PR, BASE, k0, depth2)
        row_copy(*rows2, away, n).start()
    OWN[0] = pack_top
    OWN[1] = pack_bot
    CS2[0] = jnp.where(slot < 2, pack_bot, turn(pack_top, 2))
    CS2[1] = jnp.where(slot < 2, turn(pack_top, -2), pack_bot)
    for copy in col_copies2:
        copy.start()
    for n in range(PIECES2):
        row_copy(*rows2, 1 - away, n).start()

    nearest = edge_lanes(lane, 1)

    def settle(i, carry):
        for j in range(CHUNK):
            for half in range(2):
                kappa = i * CHUNK + j
                k = half * HALF + kappa
                shift = lax.rem(2 * LANES - 4 * kappa - 2, LANES)
                V[k] = V[k] + jnp.where(nearest, turn(VC[half], shift), 0.0)
        return carry

    def lift(i, carry):
        ks, after = pl.ds(i * span, span), pl.ds(i * span + 1, span)
        W[after] = W[after] - S[ks] * (PR[after, OWN_ROWS, :] - PR[ks, OWN_ROWS, :])
        return carry

    lax.fori_loop(0, STEPS, settle, 0)
    lax.fori_loop(0, LEVELS // span, lift, 0)
    lax.fori_loop(0, LEVELS // span, inside, 0)

    for copy in col_copies2:
        copy.wait_recv()
    from_left, from_right = CR2[0], CR2[1]
    for g in range(2):
        if g == 0:
            qx = jnp.where(slot < 2, from_right, from_left)
        else:
            qx = jnp.where(slot < 2, turn(from_right, -2), turn(from_left, 2))
        edge = jnp.where(inner, EDGE[g] + HX[g] * (OWN[g] - qx), qx)
        col_effects(g, jnp.where(walled, 0.0, edge))

    chain = (zero, zero)
    for n in range(PIECES2):
        for copy in row_copies2[n]:
            copy.wait_recv()
        for half, k0 in spans(n, depth2):
            levels = pl.ds(k0, depth2)
            q_below, q_above = RR2[0, n, half, 1], RR2[1, n, half, 1]
            u_below = UH[0, levels] - HH[0, levels] * (
                read_rows(PR, BASE, k0, depth2) - RR2[0, n, half, 0]
            )
            u_above = UH[1, levels] - HH[1, levels] * (
                RR2[1, n, half, 0] - read_rows(PR, top, k0, depth2)
            )
            row_effects(k0, depth2, q_below, q_above, u_below, u_above)
        chain = eliminate((n * STEPS // PIECES2, (n + 1) * STEPS // PIECES2), chain, SRC, E, G, CORR, Y)
    for copy in sum(row_copies + row_copies2, col_copies + col_copies2):
        copy.wait_send()


def finish_kernel(
    UR, V, W, S, Y, G, M, VC,
    u_out, v_out, w_out, p_out,
    V2, W2, Q, wind_sem, sems,
):
    wind = pltpu.make_async_copy(UR.at[:, pl.ds(BASE, ROWS), :], u_out, wind_sem)
    wind.start()
    q_bot, q_top = middle(Y[HALF - 1], Y[HALF], G, M)
    nearest = edge_lanes(lax.broadcasted_iota(jnp.int32, PLANE, 1), 1)

    def settled(k, half):
        shift = lax.rem(2 * LANES - 4 * (k - half * HALF) - 2, LANES)
        return V[k] + jnp.where(nearest, turn(VC[half], shift), 0.0)

    def sweep_out(step, carry):
        q_top, q_bot = carry
        for j in range(CHUNK):
            k = HALF - 1 - step * CHUNK - j
            q_next = q_top
            q_top = Y[k] + G[k] * q_next
            Q[k] = q_top
            W2[k] = W[k + 1] - S[k] * (q_next - q_top)
            V2[k] = settled(k, 0)
            k = HALF + step * CHUNK + j
            q_before = q_bot
            q_bot = Y[k] + G[k] * q_before
            Q[k] = q_bot
            W2[k - 1] = W[k] - S[k - 1] * (q_bot - q_before)
            V2[k] = settled(k, 1)
        return q_top, q_bot

    carry = q_bot, q_top
    copies = []
    part = HALF // PARTS
    for n in range(PARTS):
        carry = lax.fori_loop(n * STEPS // PARTS, (n + 1) * STEPS // PARTS, sweep_out, carry)
        low, high = HALF - (n + 1) * part, HALF + n * part
        start, stop = max(HALF, high - 1), high + part - 1
        if n == PARTS - 1:
            W2[LEVELS - 1] = W[LEVELS] + S[LEVELS - 1] * carry[1]
            stop = LEVELS
        pieces = (
            (Q, p_out, low, low + part),
            (Q, p_out, high, high + part),
            (W2, w_out, low, low + part),
            (W2, w_out, start, stop),
            (V2, v_out, low, low + part),
            (V2, v_out, high, high + part),
        )
        for m, (source, target, begin, end) in enumerate(pieces):
            ks = pl.ds(begin, end - begin)
            copy = pltpu.make_async_copy(source.at[ks], target.at[ks], sems.at[n, m])
            copy.start()
            copies.append(copy)
    for copy in [wind] + copies:
        copy.wait()


def per_device(u, v, w, p, c, s):
    block = (LEVELS,) + PLANE
    deep = (LEVELS + 1,) + PLANE
    padded = (LEVELS, 2 * ROWS, LANES)
    pair = (2,) + PLANE
    vmem = pl.BlockSpec(memory_space=pltpu.VMEM)
    hbm = pl.BlockSpec(memory_space=pltpu.HBM)
    state = [padded, block, deep, block, block, block, PLANE, pair]
    rows1 = (2, PIECES, 2, 3, HALF // PIECES, LANES)
    rows2 = (2, PIECES2, 2, 2, HALF // PIECES2, LANES)
    halo = (2, LEVELS, LANES)
    dma = pltpu.SemaphoreType.DMA
    held = pl.pallas_call(
        exchange_kernel,
        out_shape=[jax.ShapeDtypeStruct(shape, F32) for shape in state],
        in_specs=[hbm] * 6,
        out_specs=[vmem] * len(state),
        scratch_shapes=[
            pltpu.VMEM((LEVELS + 1, 2 * ROWS, LANES), F32),
            pltpu.VMEM(block, F32),
            pltpu.VMEM(block, jnp.bfloat16),
            pltpu.VMEM(block, jnp.bfloat16),
            pltpu.VMEM(block, F32),
            pltpu.VMEM(block, F32),
            pltpu.VMEM(pair, F32),
            pltpu.VMEM(rows1, F32),
            pltpu.VMEM(rows1, F32),
            pltpu.VMEM(rows2, F32),
            pltpu.VMEM(rows2, F32),
            pltpu.VMEM(halo, F32),
            pltpu.VMEM(halo, F32),
            pltpu.VMEM((2,) + pair, F32),
            pltpu.VMEM((2,) + pair, F32),
            pltpu.VMEM(pair, F32),
            pltpu.VMEM(pair, F32),
            pltpu.VMEM(pair, F32),
            pltpu.VMEM(pair, F32),
            pltpu.VMEM(pair, F32),
            pltpu.VMEM(pair, F32),
            dma((6,)),
            dma((2, PIECES)),
            dma((2, PIECES)),
            dma((2,)),
            dma((2,)),
            dma((2, PIECES2)),
            dma((2, PIECES2)),
            dma((2,)),
            dma((2,)),
        ],
        compiler_params=pltpu.CompilerParams(
            collective_id=0, has_side_effects=True, vmem_limit_bytes=16 * 1024 * 1024
        ),
    )(*[pltpu.with_memory_space_constraint(x, pltpu.HBM) for x in (u, v, w, p, c, s)])
    return pl.pallas_call(
        finish_kernel,
        out_shape=[jax.ShapeDtypeStruct(block, F32)] * 4,
        in_specs=[vmem] * len(state),
        out_specs=[hbm] * 4,
        scratch_shapes=[
            pltpu.VMEM(block, F32),
            pltpu.VMEM(block, F32),
            pltpu.VMEM(block, F32),
            dma,
            dma((PARTS, 6)),
        ],
        compiler_params=pltpu.CompilerParams(vmem_limit_bytes=16 * 1024 * 1024),
    )(*held)


def solution(mesh):
    spec = P(None, "rows", "cols")
    return jax.shard_map(
        per_device, mesh=mesh, in_specs=(spec,) * 6, out_specs=(spec,) * 4, check_vma=False
    )
```

```python
import jax
import jax.numpy as jnp
from jax import lax
from jax.experimental import pallas as pl
from jax.experimental.pallas import tpu as pltpu
from jax.sharding import PartitionSpec as P

LEVELS = 64
HALF = LEVELS // 2
ROWS = 16
LANES = 128
BASE = 8
CHUNK = 8
STEPS = HALF // CHUNK
PIECES = 4
PIECES2 = 2
PARTS = 2
F32 = jnp.float32
OWN_ROWS = slice(BASE, BASE + ROWS)
PLANE = (ROWS, LANES)
MESH = pl.DeviceIdType.MESH


def turn(x, shift):
    return pltpu.roll(x, shift % LANES if isinstance(shift, int) else shift, x.ndim - 1)


def rows_of(ref, row, level, count):
    stride = ref.shape[1]
    return ref.reshape(ref.shape[0] * stride, LANES), pl.ds(level * stride + row, count, stride=stride)


def read_rows(ref, row, level=0, count=LEVELS):
    flat, rows = rows_of(ref, row, level, count)
    return flat[rows, :]


def write_rows(ref, row, value, level=0, count=LEVELS):
    flat, rows = rows_of(ref, row, level, count)
    flat[rows, :] = value


def edge_lanes(lane, inside):
    return (lane >= LANES - inside) | (lane < inside)


def eliminate(steps, carry, SRC, E, G, CORR, Y):
    lane = lax.broadcasted_iota(jnp.int32, PLANE, 1)
    near = edge_lanes(lane, 2)

    def body(i, carry):
        chain = list(carry)
        for j in range(CHUNK):
            for half in range(2):
                k = LEVELS - 1 - i * CHUNK - j if half else i * CHUNK + j
                shift = lax.rem(2 * LANES - 4 * (k - half * HALF) - 2, LANES)
                source = SRC[k] + jnp.where(near, turn(CORR[half], shift), 0.0)
                chain[half] = E[k] * source + G[k] * chain[half]
                Y[k] = chain[half]
        return tuple(chain)

    return lax.fori_loop(*steps, body, carry)


def middle(y_top, y_bot, G, M):
    q_bot = (y_bot + G[HALF] * y_top) * M[...]
    q_top = y_top + G[HALF - 1] * q_bot
    return q_bot, q_top


def exchange_kernel(
    u_in, v_in, w_in, p_in, c_in, s_in,
    UR, V, W, S, Y, G, M, VC,
    PR, H, C16, S16, SRC, E, CORR, RS1, RR1, RS2, RR2, UH, HH,
    CS1, CR1, CS2, CR2, OWN, HC, HX, EDGE,
    in_sems, row_send1, row_recv1, col_send1, col_recv1, row_send2, row_recv2, col_send2, col_recv2,
):
    row, col = lax.axis_index("rows"), lax.axis_index("cols")
    nrow, ncol = lax.axis_size("rows"), lax.axis_size("cols")
    up, down = lax.rem(row + 1, nrow), lax.rem(row + nrow - 1, nrow)
    right, left = lax.rem(col + 1, ncol), lax.rem(col + ncol - 1, ncol)
    targets = [(up, col), (down, col), (row, right), (row, left)]
    away = 1 - lax.rem(row, 2)

    barrier = pltpu.get_barrier_semaphore()
    for target in targets:
        pl.semaphore_signal(barrier, inc=1, device_id=target, device_id_type=MESH)

    loads = [
        pltpu.make_async_copy(c_in, C16, in_sems.at[0]),
        pltpu.make_async_copy(p_in, PR.at[pl.ds(0, LEVELS), pl.ds(BASE, ROWS), :], in_sems.at[1]),
        pltpu.make_async_copy(u_in, UR.at[:, pl.ds(BASE, ROWS), :], in_sems.at[2]),
        pltpu.make_async_copy(v_in, V, in_sems.at[3]),
        pltpu.make_async_copy(s_in, S16, in_sems.at[4]),
        pltpu.make_async_copy(w_in, W.at[pl.ds(1, LEVELS)], in_sems.at[5]),
    ]
    for load in loads:
        load.start()

    zero = jnp.zeros(PLANE, F32)
    W[0] = zero
    PR[LEVELS, OWN_ROWS, :] = zero
    no_rows = jnp.zeros((LEVELS, LANES), F32)
    for ref in (PR, UR):
        write_rows(ref, BASE - 1, no_rows)
        write_rows(ref, BASE + ROWS, no_rows)
    lane = lax.broadcasted_iota(jnp.int32, PLANE, 1)
    slot, group = lax.rem(lane, 4), lax.div(lane, 4)
    outer, inner = (slot == 0) | (slot == 3), (slot == 1) | (slot == 2)

    loads[0].wait()

    def halve(i, carry):
        k = pl.ds(i * 8, 8)
        H[k] = C16[k].astype(F32) * 0.5
        return carry

    lax.fori_loop(0, LEVELS // 8, halve, 0)

    loads[1].wait()
    loads[2].wait()

    def remote(source, landing, send_sem, recv_sem, target):
        return pltpu.make_async_remote_copy(
            src_ref=source,
            dst_ref=landing,
            send_sem=send_sem,
            recv_sem=recv_sem,
            device_id=target,
            device_id_type=MESH,
        )

    def row_copy(source, landing, send_sem, recv_sem, d, n):
        target = (lax.rem(row + nrow + 1 - 2 * d, nrow), col)
        return remote(source.at[d, n], landing.at[d, n], send_sem.at[d, n], recv_sem.at[d, n], target)

    def col_copy(source, landing, send_sem, recv_sem, d):
        return remote(source.at[d], landing.at[d], send_sem.at[d], recv_sem.at[d], targets[2 + d])

    def spans(n, depth):
        return ((0, n * depth), (1, LEVELS - (n + 1) * depth))

    top = BASE + ROWS - 1
    depth = HALF // PIECES
    for n in range(PIECES):
        for half, k0 in spans(n, depth):
            h_lo, h_hi = read_rows(H, 0, k0, depth), read_rows(H, ROWS - 1, k0, depth)
            RS1[0, n, half, 0] = read_rows(PR, top, k0, depth)
            RS1[0, n, half, 1] = read_rows(UR, top, k0, depth) + h_hi * read_rows(PR, top - 1, k0, depth)
            RS1[0, n, half, 2] = h_hi
            RS1[1, n, half, 0] = read_rows(PR, BASE, k0, depth)
            RS1[1, n, half, 1] = read_rows(UR, BASE, k0, depth) - h_lo * read_rows(PR, BASE + 1, k0, depth)
            RS1[1, n, half, 2] = h_lo

    loads[3].wait()

    def pack_first(i, carry):
        out = list(carry)
        for half in range(2):
            for j in range(CHUNK):
                kappa = i * CHUNK + j
                k = half * HALF + kappa
                mask = group == kappa
                shift = lax.rem(4 * kappa + 2, LANES)
                for n, field in enumerate((PR[k, OWN_ROWS, :], V[k], H[k])):
                    out[2 * n + half] = jnp.where(mask, turn(field, shift), out[2 * n + half])
        return tuple(out)

    packed = lax.fori_loop(0, STEPS, pack_first, (zero,) * 6)
    for g in range(2):
        pp, vp, hp = packed[g], packed[2 + g], packed[4 + g]
        OWN[g] = pp
        px = jnp.where(slot < 2, turn(pp, -2), turn(pp, 2))
        vx = jnp.where(slot < 2, turn(vp, -1), turn(vp, 1))
        hx = jnp.where(slot == 1, turn(hp, -1), jnp.where(slot == 2, -turn(hp, 1), 0.0))
        base = jnp.where(inner, vx - hx * px, px)
        CS1[0, g] = jnp.where(slot == 1, turn(hx, -1), base)
        CS1[1, g] = jnp.where(slot == 2, turn(hx, 1), base)
        HC[g] = jnp.where(
            slot == 0,
            hp * turn(hp, -1),
            jnp.where(slot == 1, -hp, jnp.where(slot == 2, hp, hp * turn(hp, 1))),
        )

    pl.semaphore_wait(barrier, 4)
    rows1 = (RS1, RR1, row_send1, row_recv1)
    row_copies = [[row_copy(*rows1, d, n) for d in range(2)] for n in range(PIECES)]
    col_copies = [col_copy(CS1, CR1, col_send1, col_recv1, d) for d in range(2)]
    for n in range(PIECES):
        row_copy(*rows1, away, n).start()
    for copy in col_copies:
        copy.start()
    for n in range(PIECES):
        row_copy(*rows1, 1 - away, n).start()

    loads[4].wait()

    def factor(i, carry):
        ratios = list(carry)
        for j in range(CHUNK):
            for half in range(2):
                k = LEVELS - 1 - i * CHUNK - j if half else i * CHUNK + j
                stiff = S16[k].astype(F32)
                S[k] = stiff
                weight = stiff * stiff
                inverse = 1.0 / (1.0 + 2.0 * weight - weight * ratios[half])
                ratios[half] = weight * inverse
                E[k] = inverse
                G[k] = ratios[half]
        return tuple(ratios)

    above, below = lax.fori_loop(0, STEPS, factor, (zero, zero))
    M[...] = 1.0 / (1.0 - above * below)
    loads[5].wait()

    span = 4
    wide_lane = lax.broadcasted_iota(jnp.int32, (span,) + PLANE, 2)
    first_lane, last_lane = wide_lane == 0, wide_lane == LANES - 1

    def across(x):
        return jnp.where(last_lane, 0.0, turn(x, -1)) - jnp.where(first_lane, 0.0, turn(x, 1))

    def inside(i, carry):
        ks = pl.ds(i * span, span)
        here, h = PR[ks, OWN_ROWS, :], H[ks]
        UR[ks, OWN_ROWS, :] = UR[ks, OWN_ROWS, :] - h * (
            PR[ks, BASE + 1 : BASE + ROWS + 1, :] - PR[ks, BASE - 1 : BASE + ROWS - 1, :]
        )
        v_new = V[ks] - h * across(here)
        V[ks] = v_new
        du = UR[ks, BASE + 1 : BASE + ROWS + 1, :] - UR[ks, BASE - 1 : BASE + ROWS - 1, :]
        lifted = S[ks] * (W[pl.ds(i * span + 1, span)] - W[ks])
        SRC[ks] = here - h * (du + across(v_new)) - lifted
        return carry

    lax.fori_loop(0, LEVELS // span, inside, 0)

    at_left, at_right = col == 0, col == ncol - 1
    walled = ((slot >= 2) & at_left) | ((slot < 2) & at_right)

    def row_effects(k0, count, p_below, p_above, u_below, u_above):
        h_lo, h_hi = read_rows(H, 0, k0, count), read_rows(H, ROWS - 1, k0, count)
        lo, hi = h_lo * p_below, h_hi * p_above
        changes = (
            (0, h_lo * u_below),
            (1, read_rows(H, 1, k0, count) * lo),
            (ROWS - 2, read_rows(H, ROWS - 2, k0, count) * hi),
            (ROWS - 1, -h_hi * u_above),
        )
        for r, change in changes:
            write_rows(SRC, r, read_rows(SRC, r, k0, count) + change, k0, count)
        write_rows(UR, BASE, read_rows(UR, BASE, k0, count) + lo, k0, count)
        write_rows(UR, top, read_rows(UR, top, k0, count) - hi, k0, count)

    def col_effects(g, edge):
        CORR[g] = HC[g] * edge
        VC[g] = HC[g] * jnp.where(slot == 1, turn(edge, 1), turn(edge, -1))

    for copy in col_copies:
        copy.wait_recv()
    for g in range(2):
        from_left, from_right = CR1[0, g], CR1[1, g]
        base = jnp.where(slot < 2, from_right, from_left)
        hx = jnp.where(
            slot == 1, turn(from_right, -1), jnp.where(slot == 2, turn(from_left, 1), 0.0)
        )
        edge = jnp.where(walled, 0.0, base + hx * OWN[g])
        HX[g] = hx
        EDGE[g] = edge
        col_effects(g, edge)

    chain = (zero, zero)
    for n in range(PIECES):
        for copy in row_copies[n]:
            copy.wait_recv()
        for half, k0 in spans(n, depth):
            levels = pl.ds(k0, depth)
            h_below, h_above = RR1[0, n, half, 2], RR1[1, n, half, 2]
            u_below = RR1[0, n, half, 1] - h_below * read_rows(PR, BASE, k0, depth)
            u_above = RR1[1, n, half, 1] + h_above * read_rows(PR, top, k0, depth)
            UH[0, levels] = u_below
            UH[1, levels] = u_above
            HH[0, levels] = h_below
            HH[1, levels] = h_above
            row_effects(k0, depth, RR1[0, n, half, 0], RR1[1, n, half, 0], u_below, u_above)
        chain = eliminate((n * STEPS // PIECES, (n + 1) * STEPS // PIECES), chain, SRC, E, G, CORR, Y)
    q_bot, q_top = middle(*chain, G, M)

    def substitute(step, carry):
        q_top, q_bot, pack_top, pack_bot = carry
        for j in range(CHUNK):
            k = HALF - 1 - step * CHUNK - j
            q_top = Y[k] + G[k] * q_top
            PR[k, OWN_ROWS, :] = q_top
            pack_top = jnp.where(group == k, turn(q_top, lax.rem(4 * k + 2, LANES)), pack_top)
            kappa = step * CHUNK + j
            k = HALF + kappa
            q_bot = Y[k] + G[k] * q_bot
            PR[k, OWN_ROWS, :] = q_bot
            pack_bot = jnp.where(group == kappa, turn(q_bot, lax.rem(4 * kappa + 2, LANES)), pack_bot)
        return q_top, q_bot, pack_top, pack_bot

    unused, unused, pack_top, pack_bot = lax.fori_loop(
        0, STEPS, substitute, (q_bot, q_top, zero, zero)
    )

    depth2 = HALF // PIECES2
    rows2 = (RS2, RR2, row_send2, row_recv2)
    row_copies2 = [[row_copy(*rows2, d, n) for d in range(2)] for n in range(PIECES2)]
    col_copies2 = [col_copy(CS2, CR2, col_send2, col_recv2, d) for d in range(2)]

    def give_rows(d, n):
        for half, k0 in spans(n, depth2):
            RS2[d, n, half, 0] = read_rows(PR, top - 1 - d * (ROWS - 3), k0, depth2)
            RS2[d, n, half, 1] = read_rows(PR, top - d * (ROWS - 1), k0, depth2)
        row_copy(*rows2, d, n).start()

    for n in range(PIECES2):
        give_rows(away, n)
    OWN[0] = pack_top
    OWN[1] = pack_bot
    CS2[0] = jnp.where(slot < 2, pack_bot, turn(pack_top, 2))
    CS2[1] = jnp.where(slot < 2, turn(pack_top, -2), pack_bot)
    for copy in col_copies2:
        copy.start()
    for n in range(PIECES2):
        give_rows(1 - away, n)

    nearest = edge_lanes(lane, 1)

    def settle(i, carry):
        for j in range(CHUNK):
            for half in range(2):
                kappa = i * CHUNK + j
                k = half * HALF + kappa
                shift = lax.rem(2 * LANES - 4 * kappa - 2, LANES)
                V[k] = V[k] + jnp.where(nearest, turn(VC[half], shift), 0.0)
        return carry

    def lift(i, carry):
        ks, after = pl.ds(i * span, span), pl.ds(i * span + 1, span)
        W[after] = W[after] - S[ks] * (PR[after, OWN_ROWS, :] - PR[ks, OWN_ROWS, :])
        return carry

    lax.fori_loop(0, STEPS, settle, 0)
    lax.fori_loop(0, LEVELS // span, lift, 0)
    lax.fori_loop(0, LEVELS // span, inside, 0)

    for copy in col_copies2:
        copy.wait_recv()
    from_left, from_right = CR2[0], CR2[1]
    for g in range(2):
        if g == 0:
            qx = jnp.where(slot < 2, from_right, from_left)
        else:
            qx = jnp.where(slot < 2, turn(from_right, -2), turn(from_left, 2))
        edge = jnp.where(inner, EDGE[g] + HX[g] * (OWN[g] - qx), qx)
        col_effects(g, jnp.where(walled, 0.0, edge))

    chain = (zero, zero)
    for n in range(PIECES2):
        for copy in row_copies2[n]:
            copy.wait_recv()
        for half, k0 in spans(n, depth2):
            levels = pl.ds(k0, depth2)
            q_below, q_above = RR2[0, n, half, 1], RR2[1, n, half, 1]
            u_below = UH[0, levels] - HH[0, levels] * (
                read_rows(PR, BASE, k0, depth2) - RR2[0, n, half, 0]
            )
            u_above = UH[1, levels] - HH[1, levels] * (
                RR2[1, n, half, 0] - read_rows(PR, top, k0, depth2)
            )
            row_effects(k0, depth2, q_below, q_above, u_below, u_above)
        chain = eliminate((n * STEPS // PIECES2, (n + 1) * STEPS // PIECES2), chain, SRC, E, G, CORR, Y)
    for copy in sum(row_copies + row_copies2, col_copies + col_copies2):
        copy.wait_send()


def finish_kernel(
    UR, V, W, S, Y, G, M, VC,
    u_out, v_out, w_out, p_out,
    V2, W2, Q, wind_sem, sems,
):
    wind = pltpu.make_async_copy(UR.at[:, pl.ds(BASE, ROWS), :], u_out, wind_sem)
    wind.start()
    q_bot, q_top = middle(Y[HALF - 1], Y[HALF], G, M)
    nearest = edge_lanes(lax.broadcasted_iota(jnp.int32, PLANE, 1), 1)

    def settled(k, half):
        shift = lax.rem(2 * LANES - 4 * (k - half * HALF) - 2, LANES)
        return V[k] + jnp.where(nearest, turn(VC[half], shift), 0.0)

    def sweep_out(step, carry):
        q_top, q_bot = carry
        for j in range(CHUNK):
            k = HALF - 1 - step * CHUNK - j
            q_next = q_top
            q_top = Y[k] + G[k] * q_next
            Q[k] = q_top
            W2[k] = W[k + 1] - S[k] * (q_next - q_top)
            V2[k] = settled(k, 0)
            k = HALF + step * CHUNK + j
            q_before = q_bot
            q_bot = Y[k] + G[k] * q_before
            Q[k] = q_bot
            W2[k - 1] = W[k] - S[k - 1] * (q_bot - q_before)
            V2[k] = settled(k, 1)
        return q_top, q_bot

    carry = q_bot, q_top
    copies = []
    part = HALF // PARTS
    for n in range(PARTS):
        carry = lax.fori_loop(n * STEPS // PARTS, (n + 1) * STEPS // PARTS, sweep_out, carry)
        low, high = HALF - (n + 1) * part, HALF + n * part
        start, stop = max(HALF, high - 1), high + part - 1
        if n == PARTS - 1:
            W2[LEVELS - 1] = W[LEVELS] + S[LEVELS - 1] * carry[1]
            stop = LEVELS
        pieces = (
            (Q, p_out, low, low + part),
            (Q, p_out, high, high + part),
            (W2, w_out, low, low + part),
            (W2, w_out, start, stop),
            (V2, v_out, low, low + part),
            (V2, v_out, high, high + part),
        )
        for m, (source, target, begin, end) in enumerate(pieces):
            ks = pl.ds(begin, end - begin)
            copy = pltpu.make_async_copy(source.at[ks], target.at[ks], sems.at[n, m])
            copy.start()
            copies.append(copy)
    for copy in [wind] + copies:
        copy.wait()


def per_device(u, v, w, p, c, s):
    block = (LEVELS,) + PLANE
    deep = (LEVELS + 1,) + PLANE
    padded = (LEVELS, 2 * ROWS, LANES)
    pair = (2,) + PLANE
    vmem = pl.BlockSpec(memory_space=pltpu.VMEM)
    hbm = pl.BlockSpec(memory_space=pltpu.HBM)
    state = [padded, block, deep, block, block, block, PLANE, pair]
    rows1 = (2, PIECES, 2, 3, HALF // PIECES, LANES)
    rows2 = (2, PIECES2, 2, 2, HALF // PIECES2, LANES)
    halo = (2, LEVELS, LANES)
    dma = pltpu.SemaphoreType.DMA
    held = pl.pallas_call(
        exchange_kernel,
        out_shape=[jax.ShapeDtypeStruct(shape, F32) for shape in state],
        in_specs=[hbm] * 6,
        out_specs=[vmem] * len(state),
        scratch_shapes=[
            pltpu.VMEM((LEVELS + 1, 2 * ROWS, LANES), F32),
            pltpu.VMEM(block, F32),
            pltpu.VMEM(block, jnp.bfloat16),
            pltpu.VMEM(block, jnp.bfloat16),
            pltpu.VMEM(block, F32),
            pltpu.VMEM(block, F32),
            pltpu.VMEM(pair, F32),
            pltpu.VMEM(rows1, F32),
            pltpu.VMEM(rows1, F32),
            pltpu.VMEM(rows2, F32),
            pltpu.VMEM(rows2, F32),
            pltpu.VMEM(halo, F32),
            pltpu.VMEM(halo, F32),
            pltpu.VMEM((2,) + pair, F32),
            pltpu.VMEM((2,) + pair, F32),
            pltpu.VMEM(pair, F32),
            pltpu.VMEM(pair, F32),
            pltpu.VMEM(pair, F32),
            pltpu.VMEM(pair, F32),
            pltpu.VMEM(pair, F32),
            pltpu.VMEM(pair, F32),
            dma((6,)),
            dma((2, PIECES)),
            dma((2, PIECES)),
            dma((2,)),
            dma((2,)),
            dma((2, PIECES2)),
            dma((2, PIECES2)),
            dma((2,)),
            dma((2,)),
        ],
        compiler_params=pltpu.CompilerParams(
            collective_id=0, has_side_effects=True, vmem_limit_bytes=16 * 1024 * 1024
        ),
    )(*[pltpu.with_memory_space_constraint(x, pltpu.HBM) for x in (u, v, w, p, c, s)])
    return pl.pallas_call(
        finish_kernel,
        out_shape=[jax.ShapeDtypeStruct(block, F32)] * 4,
        in_specs=[vmem] * len(state),
        out_specs=[hbm] * 4,
        scratch_shapes=[
            pltpu.VMEM(block, F32),
            pltpu.VMEM(block, F32),
            pltpu.VMEM(block, F32),
            dma,
            dma((PARTS, 6)),
        ],
        compiler_params=pltpu.CompilerParams(vmem_limit_bytes=16 * 1024 * 1024),
    )(*held)


def solution(mesh):
    spec = P(None, "rows", "cols")
    return jax.shard_map(
        per_device, mesh=mesh, in_specs=(spec,) * 6, out_specs=(spec,) * 4, check_vma=False
    )
```
